256 devices in a mesh: dp: 32 (over z_hi, x, core), mp: 8 (over z_lo, y).
Axes of the slice: x: 4, y: 4, z: 8 (z_hi: 4, z_lo: 2; z = z_hi * 2 + z_lo), core: 2. Of those that a mesh axis runs over, the one named last changes fastest.
Arguments:
- tokens: bfloat16 [128, 64, 4096], P('dp', None, 'mp'), may hold values from -40 to 40
- groups: int32 [64, 128], P('dp'), may hold values from 0 to 127, each once within a row
- router: bfloat16 [4096, 64], P('mp'), may hold values from -0.5 to 0.5
- w_in: bfloat16 [65536, 4096], P(('mp', 'dp')), may hold values from -0.09375 to 0.09375
- w_out: bfloat16 [65536, 4096], P(('mp', 'dp')), may hold values from -0.75 to 0.75
- cotangent: bfloat16 [128, 64, 4096], P('dp', None, 'mp'), may hold values from -6 to 6
Outputs:
- mixed_out: bfloat16 [128, 64, 4096], P('dp', None, 'mp')
- tokens_grad: bfloat16 [128, 64, 4096], P('dp', None, 'mp')
- router_grad: float32 [4096, 64], P('mp')
- w_in_grad: bfloat16 [65536, 4096], P(('mp', 'dp'))
- w_out_grad: bfloat16 [65536, 4096], P(('mp', 'dp'))
The draws below stay inside these ranges and needn't reach their ends.
Inputs may be any that keep to these rules, and one draw needn't show every extreme that they name: `groups`: each row is a permutation of the 128 sequences.
All inputs are finite; a program needn't handle non-finite values.
Results may differ from the reference program's by a relative error of at most 0.035.
Values may be sent and summed in bfloat16 or wider, within the bound.
A program may use at most 128 MiB of HBM per device.

```python
import math
import jax
import jax.numpy as jnp
from jax import lax

D = 4096
FF = 1024
GROUP = 32
SPLIT = 4
SEQS = 128
LEN = 64
EXPERTS = 64


def router_base(key):
    values = 2.0 * jax.random.normal(key, (D, EXPERTS), jnp.float32) / math.sqrt(D)
    return jnp.clip(values, -0.5, 0.5)


def draw_router(key, part):
    shared = router_base(key)
    return shared.astype(jnp.bfloat16)


def draw_tokens(key, part):
    key = jax.random.fold_in(key, 3)
    key_base = jax.random.fold_in(key, 0)
    values = jax.random.normal(key_base, (SEQS, LEN, D), jnp.float32)
    return jnp.clip(values, -40.0, 40.0).astype(jnp.bfloat16)


def block_levels(rng, dims, cuts, low, largest):
    loudness = 1.0
    for position, parts in cuts:
        heights = jax.random.uniform(jax.random.fold_in(jax.random.fold_in(rng, 6), position), (parts,), jnp.float32, low / len(cuts), largest / len(cuts))
        loudness = loudness * jnp.repeat(jnp.exp(heights), dims[position] // parts).reshape((-1,) + (1,) * (len(dims) - 1 - position))
    return loudness


def scatter_about(key, shape, width, bound, cuts=(), held_as=jnp.bfloat16):
    array = width * jax.random.normal(key, shape, jnp.float32)
    if cuts:
        array = array * block_levels(key, shape, cuts, -0.22, 0.18)
    return jnp.clip(array, -bound, bound).astype(held_as)


def setup_inputs(seed: int = 0) -> dict:
    key_list = jax.random.split(jax.random.key(seed), 7)
    return {
        "tokens": draw_tokens(jax.random.fold_in(key_list[6], 71), 0),
        "groups": jax.vmap(lambda own: jax.random.permutation(own, SEQS))(jax.random.split(key_list[1], LEN)).reshape((LEN, SEQS)).astype(jnp.int32),
        "router": draw_router(jax.random.fold_in(key_list[6], 71), 0),
        "w_in": scatter_about(key_list[3], (EXPERTS * FF, D), D ** -0.5, 0.09375, ((0, 256),)),
        "w_out": scatter_about(key_list[4], (EXPERTS * FF, D), (FF // 16) ** -0.5, 0.75, ((0, 256),)),
        "cotangent": scatter_about(key_list[5], (SEQS, LEN, D), 1.0, 6.0, ((0, 32), (2, 8))),
    }


def group_rows(full_rows, groups):
    turned = jnp.swapaxes(full_rows, 0, 1)
    picked = jnp.take_along_axis(turned, groups[:, :, None], axis=1)
    return picked.reshape(-1, GROUP, full_rows.shape[2])


def ungroup_rows(grouped, groups):
    positions, seq_count = groups.shape
    flat_rows = grouped.reshape(positions, seq_count, grouped.shape[-1])
    row_ids = jnp.arange(positions, dtype=jnp.int32)[:, None]
    order_ids = jnp.broadcast_to(jnp.arange(seq_count, dtype=jnp.int32)[None, :], groups.shape)
    inverse = jnp.zeros_like(groups).at[row_ids, groups].set(order_ids)
    return jnp.swapaxes(jnp.take_along_axis(flat_rows, inverse[:, :, None], axis=1), 0, 1)


def block_sum(active, matrix):
    group_count = active.shape[0]
    feat_width = matrix.shape[1]
    pieces = active.reshape(group_count, SPLIT, -1).astype(jnp.float32)
    mat_pieces = matrix.reshape(SPLIT, -1, feat_width).astype(jnp.float32)
    part_terms = jnp.einsum("gqf,qfd->qgd", pieces, mat_pieces).astype(jnp.bfloat16)
    return jnp.sum(part_terms.astype(jnp.float32), axis=0).astype(jnp.bfloat16)


def reference(tokens, groups, router, w_in, w_out, cotangent):
    grouped_tok = group_rows(tokens, groups)
    grouped_cot = group_rows(cotangent, groups)
    group_count = grouped_tok.shape[0]
    feat_width = grouped_tok.shape[2]
    experts = router.shape[1]
    hidden = w_in.shape[0] // experts
    logits = jnp.dot(grouped_tok.reshape(-1, feat_width), router, preferred_element_type=jnp.float32)
    logits = logits.reshape(group_count, GROUP, experts)
    weights = jax.nn.softmax(logits, axis=1)
    weight_bf = weights.astype(jnp.bfloat16)
    tok_f = grouped_tok.astype(jnp.float32)
    cot_f = grouped_cot.astype(jnp.float32)
    w_first = w_in.reshape(experts, hidden, feat_width)
    w_second = w_out.reshape(experts, hidden, feat_width)
    weight_cols = jnp.moveaxis(weight_bf, 2, 0)

    def one_expert(state_pair, inputs):
        out_acc, dtok_acc = state_pair
        weight_col, first_mat, second_mat = inputs
        weight_f = weight_col.astype(jnp.float32)
        mixed_rows = jnp.einsum("gt,gtd->gd", weight_f, tok_f).astype(jnp.bfloat16)
        pre_act = jnp.dot(mixed_rows, first_mat.T, preferred_element_type=jnp.float32)
        active = jax.nn.silu(pre_act).astype(jnp.bfloat16)
        produced = block_sum(active, second_mat)
        back_rows = jnp.einsum("gt,gtd->gd", weight_f, cot_f).astype(jnp.bfloat16)
        d_active = jnp.dot(back_rows, second_mat.T, preferred_element_type=jnp.float32)
        grad_second = jnp.dot(active.T, back_rows, preferred_element_type=jnp.float32).astype(jnp.bfloat16)
        gate_sig = jax.nn.sigmoid(pre_act)
        d_pre = (d_active * gate_sig * (1.0 + pre_act * (1.0 - gate_sig))).astype(jnp.bfloat16)
        grad_first = jnp.dot(d_pre.T, mixed_rows, preferred_element_type=jnp.float32).astype(jnp.bfloat16)
        d_mixed = block_sum(d_pre, first_mat)
        produced_f = produced.astype(jnp.float32)
        dmixed_f = d_mixed.astype(jnp.float32)
        out_acc = out_acc + weight_f[:, :, None] * produced_f[:, None, :]
        dtok_acc = dtok_acc + weight_f[:, :, None] * dmixed_f[:, None, :]
        d_weight = jnp.einsum("gtd,gd->gt", cot_f, produced_f) + jnp.einsum("gtd,gd->gt", tok_f, dmixed_f)
        return (out_acc, dtok_acc), (d_weight, grad_first, grad_second)

    zeros_rows = jnp.zeros((group_count, GROUP, feat_width), jnp.float32)
    (out_acc, dtok_acc), (d_weights, grads_first, grads_second) = lax.scan(
        one_expert, (zeros_rows, zeros_rows), (weight_cols, w_first, w_second))
    d_weight = jnp.moveaxis(d_weights, 0, 2)
    d_logit = weights * (d_weight - jnp.sum(weights * d_weight, axis=1, keepdims=True))
    d_logit_bf = d_logit.astype(jnp.bfloat16)
    d_tokens = dtok_acc + jnp.einsum("gte,de->gtd", d_logit_bf.astype(jnp.float32), router.astype(jnp.float32))
    router_grad = jnp.einsum("gtd,gte->de", tok_f, d_logit_bf.astype(jnp.float32))
    mixed_out = ungroup_rows(out_acc.astype(jnp.bfloat16), groups)
    tokens_grad = ungroup_rows(d_tokens.astype(jnp.bfloat16), groups)
    w_in_grad = grads_first.reshape(experts * hidden, feat_width)
    w_out_grad = grads_second.reshape(experts * hidden, feat_width)
    return (mixed_out, tokens_grad, router_grad, w_in_grad, w_out_grad)
```

```python
import jax
import jax.numpy as jnp
from jax import lax
from jax.experimental import pallas as pl
from jax.experimental.pallas import tpu as pltpu
from jax.sharding import PartitionSpec as P

MESH = pl.DeviceIdType.MESH
BF = jnp.bfloat16
F32 = jnp.float32
NDP = 32
NMP = 8
CH = 4

NT = (((1,), (1,)), ((), ()))
TN = (((0,), (0,)), ((), ()))


def dot(a, b):
    return jnp.dot(a, b, preferred_element_type=F32)


def dot_nt(a, b):
    return lax.dot_general(a, b, NT, preferred_element_type=F32)


def dot_tn(a, b):
    return lax.dot_general(a, b, TN, preferred_element_type=F32)


def iota(shape, dim):
    return lax.broadcasted_iota(jnp.int32, shape, dim)


def wait_bytes(view, sem):
    pltpu.make_async_copy(view, view, sem).wait()


(S_X, S_C, S_L, S_MIX, S_M, S_B, S_QSIB, S_QX, S_QF, S_BSIB, S_BX, S_BF) = range(12)
S_PSIB, S_PX, S_PA, S_DSIB, S_DX, S_DA, S_O, S_DW, S_DL, S_G, S_R, S_RG = range(12, 24)
N_SEND = 24
R_X, R_C, R_L, R_MIX, R_M, R_B, R_QSIB, R_QX, R_QF, R_BSIB, R_BX, R_BF = (0, 1, 2, 3, 4, 5, 6, 7, 11, 15, 16, 20)
R_PSIB, R_PX, R_PA, R_DSIB, R_DX, R_DA, R_O, R_DW, R_DL, R_G, R_R, R_RG = (24, 28, 32, 33, 37, 41, 42, 43, 44, 45, 46, 47)
N_RECV = 48


def kernel(tok, cot, grp, rt, w_in, w_out,
           o_mix, o_grad, o_router, o_win, o_wout,
           xs, cs, xin, cin, lsend, lin, mixsend, mixall, amat, mbuf, bbuf,
           g_fwd, g_back, xf, cf, wi, wo, pb, sb, xsum, xr, rb, pin,
           pb2, sb2, xsum2, xr2, rb2, din, osend, oin, gsend, gin,
           wlsend, wlin, dlsend, dlall, bacc, dtok, rsend, rin, rall, rsum, acc, gi, go,
           send, recv, wsem):
    me_p = lax.axis_index("dp")
    me_m = lax.axis_index("mp")
    p4 = me_p // 4
    q = me_p % 4
    u = me_m * 8 + p4
    sib = me_p + 1 - 2 * (me_p % 2)
    xnb = me_p + 2 - 4 * (q // 2)
    q_sib = q + 1 - 2 * (q % 2)
    q_x = q + 2 - 4 * (q // 2)
    q_d = q_sib + 2 - 4 * (q_sib // 2)

    def rcopy(src, dst, s, r, dev):
        return pltpu.make_async_remote_copy(
            src_ref=src, dst_ref=dst, send_sem=send.at[s], recv_sem=recv.at[r],
            device_id=dev, device_id_type=MESH)

    load_wi = pltpu.make_async_copy(w_in, wi, wsem.at[0])
    load_wo = pltpu.make_async_copy(w_out, wo, wsem.at[1])
    load_wi.start()
    load_wo.start()

    bar = pltpu.get_barrier_semaphore()

    def sig_row(k, c):
        pl.semaphore_signal(bar, inc=1, device_id=((me_p + k) % NDP, me_m), device_id_type=MESH)
        return c

    lax.fori_loop(1, NDP, sig_row, 0)

    def sig_class(k, c):
        col = (me_m + 1 + k // 8) % NMP
        pl.semaphore_signal(bar, inc=1, device_id=((k % 8) * 4 + q, col), device_id_type=MESH)
        return c

    lax.fori_loop(0, 56, sig_class, 0)

    r_i = iota((256, 256), 0)
    c_i = iota((256, 256), 1)
    src_row = ((r_i // 2) % 4) * 64 + (r_i // 8) * 2 + r_i % 2
    perm = (c_i == src_row).astype(F32).astype(BF)

    def blocks(ref, out):
        rows = ref[...].reshape(256, 512)
        for h in range(2):
            res = dot(perm, rows[:, h * 256:(h + 1) * 256])
            out[:, h * 8:(h + 1) * 8, :] = res.reshape(32, 8, 256).astype(BF)

    def send_row(src, dst, s, r):
        def body(k, c):
            peer = (me_p + k) % NDP
            rcopy(src.at[peer], dst.at[me_p], s, r, (peer, me_m)).start()
            return c
        lax.fori_loop(1, NDP, body, 0)

    def send_col(src, dst, s, r, spread):
        def body(k, c):
            peer = (me_m + k) % NMP
            part = src.at[peer] if spread else src
            rcopy(part, dst.at[me_m], s, r, (me_p, peer)).start()
            return c
        lax.fori_loop(1, NMP, body, 0)

    blocks(tok, xs)
    pl.semaphore_wait(bar, 31 + 56)
    send_row(xs, xin, S_X, R_X)
    blocks(cot, cs)
    send_row(cs, cin, S_C, R_C)
    xin[me_p] = xs[me_p]
    cin[me_p] = cs[me_p]

    t_i = iota((256, 128), 0)
    l_i = iota((256, 128), 1)
    order = jnp.where(t_i % 2 == 0, grp[0:1, :], grp[1:2, :])
    hit = (order == t_i // 2).astype(F32).astype(BF)
    g_i = iota((8, 128), 0)
    s_i = iota((8, 128), 1)
    pick = (s_i // 32 == g_i % 4).astype(F32).astype(BF)
    own_pos = (iota((8, 256), 1) % 2 == iota((8, 256), 0) // 4).astype(F32)
    m8 = dot_nt(pick, hit) * own_pos

    def half(ref, h, rows):
        return ref[:, h * 8:(h + 1) * 8, :].astype(F32).reshape(rows, ref.shape[-1]).astype(BF)

    wait_bytes(xin.at[pl.ds(0, 31)], recv.at[R_X])
    x0, x1 = half(xin, 0, 256), half(xin, 1, 256)
    r0, r1 = rt[:, 0:256], rt[:, 256:512]
    lsend[...] = (dot_nt(r0, x0) + dot_nt(r1, x1)).reshape(8, 8, 256)
    send_col(lsend, lin, S_L, R_L, True)
    lin[me_m] = lsend[me_m]
    wait_bytes(lin.at[pl.ds(0, 7)], recv.at[R_L])
    logit = jnp.sum(lin[...], axis=0)
    big = jnp.full((8, 256), -jnp.inf, F32)
    peak = jnp.zeros((8, 256), F32)
    for g in range(8):
        inside = jnp.broadcast_to(m8[g:g + 1, :] > 0.5, (8, 256))
        top = jnp.max(jnp.where(inside, logit, big), axis=1, keepdims=True)
        peak = jnp.where(inside, top, peak)
    ex = jnp.exp(logit - peak)
    den = jnp.zeros((8, 256), F32)
    for g in range(8):
        mask = m8[g:g + 1, :]
        den = den + mask * jnp.sum(ex * mask, axis=1, keepdims=True)
    mix_own = ex / den
    mixsend[0:8, :] = mix_own[:, 0:128].astype(BF)
    mixsend[8:16, :] = mix_own[:, 128:256].astype(BF)
    send_col(mixsend, mixall, S_MIX, R_MIX, False)
    mixall[me_m] = mixsend[...]
    wait_bytes(mixall.at[pl.ds(0, 7)], recv.at[R_MIX])

    spread = (iota((512, 64), 0) // 8 == iota((512, 64), 1)).astype(F32).astype(BF)
    for h in range(2):
        wide = dot(spread, half(mixall, h, 64)).reshape(64, 8, 128)
        sel = wide * m8[:, h * 128:(h + 1) * 128][None]
        amat[:, h * 128:(h + 1) * 128] = sel.reshape(512, 128).astype(BF)

    def send_class(src, dst, s, r):
        def body(k, c):
            v = (u + k) % 64
            rcopy(src.at[v], dst, s, r, ((v % 8) * 4 + q, v // 8)).start()
            return c
        lax.fori_loop(1, 64, body, 0)

    def mixing(rows, buf, dst, s, r):
        for h in range(2):
            res = dot(amat[...], rows[h])
            buf[:, h * 8:(h + 1) * 8, :] = res.reshape(64, 8, 256).astype(BF)
        send_class(buf, dst.at[q, u], s, r)
        dst[q, u] = buf[u]

    mixing((x0, x1), mbuf, g_fwd, S_M, R_M)
    wait_bytes(cin.at[pl.ds(0, 31)], recv.at[R_C])
    mixing((half(cin, 0, 256), half(cin, 1, 256)), bbuf, g_back, S_B, R_B)

    def quad_start(g, r_own, s_sib, r_sib, s_x, r_x):
        wait_bytes(g.at[0, pl.ds(0, 63)], recv.at[r_own])

        def body(j, c):
            part = g.at[q, pl.ds(j * 16, 16)]
            rcopy(part, part, s_x, r_x + j, (xnb, me_m)).start()
            return c
        lax.fori_loop(0, CH, body, 0)
        rcopy(g.at[q], g.at[q], s_sib, r_sib, (sib, me_m)).start()

    def quad_forward(g, r_x, s_f, r_f):
        def body(j, c):
            part = g.at[q_x, pl.ds(j * 16, 16)]
            wait_bytes(part, recv.at[r_x + j])
            rcopy(part, part, s_f, r_f + j, (sib, me_m)).start()
            return c
        lax.fori_loop(0, CH, body, 0)

    def quad_done(g, r_sib, r_f):
        wait_bytes(g.at[q_sib], recv.at[r_sib])

        def body(j, c):
            wait_bytes(g.at[q_d, pl.ds(j * 16, 16)], recv.at[r_f + j])
            return c
        lax.fori_loop(0, CH, body, 0)

    def project(g, flat, w):
        acc[...] = jnp.zeros((256, 256), F32)

        def body(m, c):
            for h in range(2):
                col = pl.multiple_of(m * 512 + h * 256, 256)
                part = g[:, pl.ds(m * 8, 8), h * 8:(h + 1) * 8, :].astype(F32).reshape(256, 256).astype(BF)
                flat[:, pl.ds(col, 256)] = part
                acc[...] += dot_nt(part, w[:, pl.ds(col, 256)])
            return c
        lax.fori_loop(0, NMP, body, 0)
        return acc[...]

    def parts(rows, w, buf, landing, s, r):
        def chunk(j, c):
            jj = (me_m // 2 + j) % CH

            def one(i, c2):
                m = jj * 2 + i
                for h in range(2):
                    col = pl.multiple_of(m * 512 + h * 256, 256)
                    res = dot(rows, w[:, pl.ds(col, 256)])
                    buf[:, pl.ds(m * 8, 8), h * 8:(h + 1) * 8, :] = res.reshape(4, 8, 8, 256).astype(BF)
                return c2
            lax.fori_loop(0, 2, one, 0)
            span = pl.ds(jj * 16, 16)
            rcopy(buf.at[q_d, span], landing.at[1, span], s, r + j, (sib, me_m)).start()
            rcopy(buf.at[q_sib, span], landing.at[0, span], s, r + j, (sib, me_m)).start()
            return c
        lax.fori_loop(0, CH, chunk, 0)

    def pair_sums(buf, landing, out, far, r_sib, s, r):
        def chunk(j, c):
            jj = (me_m // 2 + j) % CH
            span = pl.ds(jj * 16, 16)
            wait_bytes(landing.at[pl.ds(0, 2), span], recv.at[r_sib + j])
            out[span] = (buf[q_x, span].astype(F32) + landing[1, span].astype(F32)).astype(BF)
            rcopy(out.at[span], far.at[span], s, r + j, (xnb, me_m)).start()
            return c
        lax.fori_loop(0, CH, chunk, 0)

    def totals(buf, landing, far, out, home, r_x, s, r):
        def finish(jj, j):
            span = pl.ds(jj * 16, 16)
            wait_bytes(far.at[span], recv.at[r_x + j])
            out[span] = (buf[q, span].astype(F32) + landing[0, span].astype(F32)
                         + far[span].astype(F32)).astype(BF)

        def post(v):
            rcopy(out.at[v], home.at[u], s, r, ((v % 8) * 4 + q, v // 8)).start()

        first = me_m // 2
        finish(first, 0)
        w = u % 16

        def near(k, c):
            post(first * 16 + (w + k) % 16)
            return c
        lax.fori_loop(1, 16, near, 0)
        home[u] = out[u]

        def chunk(j, c):
            jj = (first + j) % CH
            finish(jj, j)

            def each(k, c2):
                post(jj * 16 + (w + k) % 16)
                return c2
            lax.fori_loop(0, 16, each, 0)
            return c
        lax.fori_loop(1, CH, chunk, 0)

    quad_start(g_fwd, R_M, S_QSIB, R_QSIB, S_QX, R_QX)
    quad_forward(g_fwd, R_QX, S_QF, R_QF)
    quad_start(g_back, R_B, S_BSIB, R_BSIB, S_BX, R_BX)
    load_wi.wait()
    load_wo.wait()
    quad_done(g_fwd, R_QSIB, R_QF)
    pre = project(g_fwd, xf, wi)
    sig = 1.0 / (1.0 + jnp.exp(-pre))
    act_f = pre * sig
    slope = sig * (1.0 + pre * (1.0 - sig))
    dtok[:, 0:256] = slope
    active = act_f.astype(BF)
    parts(active, wo, pb, sb, S_PSIB, R_PSIB)
    quad_forward(g_back, R_BX, S_BF, R_BF)
    pair_sums(pb, sb, xsum, xr, R_PSIB, S_PX, R_PX)
    quad_done(g_back, R_BSIB, R_BF)
    d_pre_f = project(g_back, cf, wo) * dtok[:, 0:256]
    d_pre = d_pre_f.astype(BF)
    parts(d_pre, wi, pb2, sb2, S_DSIB, R_DSIB)
    totals(pb, sb, xr, rb, pin, R_PX, S_PA, R_PA)
    pair_sums(pb2, sb2, xsum2, xr2, R_DSIB, S_DX, R_DX)
    active_t = act_f.T.astype(BF)
    d_pre_t = d_pre_f.T.astype(BF)

    def weight_grads(m, c):
        col = pl.ds(pl.multiple_of(m * 512, 512), 512)
        go[:, col] = dot(active_t, cf[:, col]).astype(BF)
        gi[:, col] = dot(d_pre_t, xf[:, col]).astype(BF)
        return c
    lax.fori_loop(0, NMP, weight_grads, 0)
    store_wi = pltpu.make_async_copy(gi, o_win, wsem.at[2])
    store_wo = pltpu.make_async_copy(go, o_wout, wsem.at[3])
    store_wi.start()
    store_wo.start()
    totals(pb2, sb2, xr2, rb2, din, R_DX, S_DA, R_DA)

    wait_bytes(pin.at[pl.ds(0, 63)], recv.at[R_PA])
    for h in range(2):
        rows = half(pin, h, 512)
        res = dot_tn(amat[...], rows)
        osend[:, h * 8:(h + 1) * 8, :] = res.reshape(32, 8, 256).astype(BF)
        part = dot_nt(rows, half(cin, h, 256))
        if h == 0:
            bacc[...] = part
        else:
            bacc[...] += part
    send_row(osend, oin, S_O, R_O)
    oin[me_p] = osend[me_p]

    wait_bytes(din.at[pl.ds(0, 63)], recv.at[R_DA])
    for h in range(2):
        bacc[...] += dot_nt(half(din, h, 512), half(xin, h, 256))
    wlsend[...] = jnp.sum(bacc[...].reshape(64, 8, 256) * m8[None], axis=1).reshape(8, 8, 256)
    send_col(wlsend, wlin, S_DW, R_DW, True)
    wlin[me_m] = wlsend[me_m]
    for h in range(2):
        dtok[:, h * 256:(h + 1) * 256] = dot_tn(amat[...], half(din, h, 512))
    wait_bytes(wlin.at[pl.ds(0, 7)], recv.at[R_DW])
    d_weight = jnp.sum(wlin[...], axis=0)
    prod = mix_own * d_weight
    mean = jnp.zeros((8, 256), F32)
    for g in range(8):
        mask = m8[g:g + 1, :]
        mean = mean + mask * jnp.sum(prod * mask, axis=1, keepdims=True)
    d_logit = mix_own * (d_weight - mean)
    dlsend[0:8, :] = d_logit[:, 0:128].astype(BF)
    dlsend[8:16, :] = d_logit[:, 128:256].astype(BF)
    send_col(dlsend, dlall, S_DL, R_DL, False)
    dlall[me_m] = dlsend[...]
    wait_bytes(dlall.at[pl.ds(0, 7)], recv.at[R_DL])
    dl = jnp.concatenate([half(dlall, 0, 64), half(dlall, 1, 64)], axis=1)
    for h in range(2):
        res = dtok[:, h * 256:(h + 1) * 256] + dot_tn(dl, rt[:, h * 256:(h + 1) * 256])
        gsend[:, h * 8:(h + 1) * 8, :] = res.reshape(32, 8, 256).astype(BF)
    send_row(gsend, gin, S_G, R_G)
    gin[me_p] = gsend[me_p]
    for h in range(2):
        part = dot(dl, half(xin, h, 256))
        for k in range(2):
            tile = part[:, k * 128:(k + 1) * 128].reshape(8, 8, 128)
            for e in range(8):
                rsend[e * 4 + h * 2 + k] = tile[e]
    send_row(rsend, rin, S_R, R_R)
    rin[me_p] = rsend[me_p]
    wait_bytes(rin.at[pl.ds(0, 31)], recv.at[R_R])
    rsum[...] = jnp.sum(rin[...], axis=0)

    def share(k, c):
        peer = (me_p + k) % NDP
        rcopy(rsum, rall.at[me_p], S_RG, R_RG, (peer, me_m)).start()
        return c
    lax.fori_loop(1, NDP, share, 0)
    rall[me_p] = rsum[...]

    def place(src, out):
        for h in range(2):
            res = dot_tn(perm, half(src, h, 256)).astype(BF)
            out[:, :, h * 256:(h + 1) * 256] = res.reshape(4, 64, 256)

    wait_bytes(oin.at[pl.ds(0, 31)], recv.at[R_O])
    place(oin, o_mix)
    wait_bytes(gin.at[pl.ds(0, 31)], recv.at[R_G])
    place(gin, o_grad)
    wait_bytes(rall.at[pl.ds(0, 31)], recv.at[R_RG])
    for e in range(8):
        for k in range(4):
            o_router[e * 8:(e + 1) * 8, k * 128:(k + 1) * 128] = rall[e * 4 + k]

    for view, s in (
        (xs.at[pl.ds(0, 31)], S_X), (cs.at[pl.ds(0, 31)], S_C), (lin.at[pl.ds(0, 7)], S_L),
        (mixall.at[pl.ds(0, 7)], S_MIX), (mbuf.at[pl.ds(0, 63)], S_M), (bbuf.at[pl.ds(0, 63)], S_B),
        (g_fwd.at[0], S_QSIB), (g_fwd.at[0], S_QX), (g_fwd.at[0], S_QF),
        (g_back.at[0], S_BSIB), (g_back.at[0], S_BX), (g_back.at[0], S_BF),
        (sb, S_PSIB), (xsum, S_PX), (rb.at[pl.ds(0, 63)], S_PA),
        (sb2, S_DSIB), (xsum2, S_DX), (rb2.at[pl.ds(0, 63)], S_DA),
        (osend.at[pl.ds(0, 31)], S_O), (wlin.at[pl.ds(0, 7)], S_DW), (dlall.at[pl.ds(0, 7)], S_DL),
        (gsend.at[pl.ds(0, 31)], S_G), (rsend.at[pl.ds(0, 31)], S_R), (rall.at[pl.ds(0, 31)], S_RG),
    ):
        wait_bytes(view, send.at[s])
    store_wi.wait()
    store_wo.wait()


def per_device(tokens, groups, router, w_in, w_out, cotangent):
    vm = lambda shape, dt=BF: pltpu.VMEM(shape, dt)
    blk32, blk64 = (32, 16, 256), (64, 16, 256)
    scratch = [
        vm(blk32), vm(blk32), vm(blk32), vm(blk32),
        vm((8, 8, 256), F32), vm((8, 8, 256), F32), vm((16, 128)), vm((8, 16, 128)), vm((512, 256)),
        vm(blk64), vm(blk64),
        vm((4,) + blk64), vm((4,) + blk64), vm((256, 4096)), vm((256, 4096)),
        vm((256, 4096)), vm((256, 4096)),
        vm((4,) + blk64), vm((2,) + blk64), vm(blk64), vm(blk64), vm(blk64), vm(blk64),
        vm((4,) + blk64), vm((2,) + blk64), vm(blk64), vm(blk64), vm(blk64), vm(blk64),
        vm(blk32), vm(blk32), vm(blk32), vm(blk32),
        vm((8, 8, 256), F32), vm((8, 8, 256), F32), vm((16, 128)), vm((8, 16, 128)), vm((512, 256), F32), vm((256, 512), F32),
        vm((32, 8, 128), F32), vm((32, 8, 128), F32), vm((32, 8, 128), F32), vm((8, 128), F32),
        vm((256, 256), F32), vm((256, 4096)), vm((256, 4096)),
        pltpu.SemaphoreType.DMA((N_SEND,)), pltpu.SemaphoreType.DMA((N_RECV,)),
        pltpu.SemaphoreType.DMA((4,)),
    ]
    in_vmem = pl.BlockSpec(memory_space=pltpu.VMEM)
    anywhere = pl.BlockSpec(memory_space=pl.ANY)
    mixed_out, tokens_grad, router_t, g_in, g_out = pl.pallas_call(
        kernel,
        out_shape=(
            jax.ShapeDtypeStruct((4, 64, 512), BF),
            jax.ShapeDtypeStruct((4, 64, 512), BF),
            jax.ShapeDtypeStruct((64, 512), F32),
            jax.ShapeDtypeStruct((256, 4096), BF),
            jax.ShapeDtypeStruct((256, 4096), BF),
        ),
        in_specs=[in_vmem, in_vmem, in_vmem, in_vmem, anywhere, anywhere],
        out_specs=[in_vmem, in_vmem, in_vmem, anywhere, anywhere],
        scratch_shapes=scratch,
        compiler_params=pltpu.CompilerParams(
            collective_id=0, has_side_effects=True, vmem_limit_bytes=56 * 1024 * 1024),
        cost_estimate=pl.CostEstimate(flops=4 * 10**9, bytes_accessed=10**7, transcendentals=10**5),
    )(tokens, cotangent, groups, router.T, w_in, w_out)
    return mixed_out, tokens_grad, router_t.T, g_in, g_out


def solution(mesh):
    return jax.shard_map(
        per_device,
        mesh=mesh,
        in_specs=(
            P("dp", None, "mp"),
            P("dp", None),
            P("mp", None),
            P(("mp", "dp"), None),
            P(("mp", "dp"), None),
            P("dp", None, "mp"),
        ),
        out_specs=(
            P("dp", None, "mp"),
            P("dp", None, "mp"),
            P("mp", None),
            P(("mp", "dp"), None),
            P(("mp", "dp"), None),
        ),
        check_vma=False,
    )
```

```python
import jax
import jax.numpy as jnp
from jax import lax
from jax.experimental import pallas as pl
from jax.experimental.pallas import tpu as pltpu
from jax.sharding import PartitionSpec as P

MESH = pl.DeviceIdType.MESH
BF = jnp.bfloat16
F32 = jnp.float32
NDP = 32
NMP = 8
CH = 4

NT = (((1,), (1,)), ((), ()))
TN = (((0,), (0,)), ((), ()))


def dot(a, b):
    return jnp.dot(a, b, preferred_element_type=F32)


def dot_nt(a, b):
    return lax.dot_general(a, b, NT, preferred_element_type=F32)


def dot_tn(a, b):
    return lax.dot_general(a, b, TN, preferred_element_type=F32)


def iota(shape, dim):
    return lax.broadcasted_iota(jnp.int32, shape, dim)


def wait_bytes(view, sem):
    pltpu.make_async_copy(view, view, sem).wait()


(S_X, S_C, S_L, S_MIX, S_M, S_B, S_QSIB, S_QX, S_QF, S_BSIB, S_BX, S_BF) = range(12)
S_PSIB, S_PX, S_PA, S_DSIB, S_DX, S_DA, S_O, S_DW, S_DL, S_G, S_R, S_RG = range(12, 24)
N_SEND = 24
R_X, R_C, R_L, R_MIX, R_PA, R_DA, R_O, R_DW, R_DL, R_G, R_R, R_RG = range(12)
(R_M, R_B, R_QSIB, R_QX, R_QF, R_BSIB, R_BX, R_BF, R_PSIB, R_PX, R_DSIB, R_DX) = range(12, 60, 4)
N_RECV = 60


def kernel(tok, cot, grp, rt, w_in, w_out,
           o_mix, o_grad, o_router, o_win, o_wout,
           xs, cs, xin, cin, lsend, lin, mixsend, mixall, amat, mbuf, bbuf,
           g_fwd, g_back, xf, cf, wi, wo, pb, sb, xsum, xr, rb, pin,
           pb2, sb2, xsum2, xr2, rb2, din, osend, oin, gsend, gin,
           wlsend, wlin, dlsend, dlall, bacc, dtok, rsend, rin, rall, rsum, acc, gi, go,
           send, recv, wsem):
    me_p = lax.axis_index("dp")
    me_m = lax.axis_index("mp")
    p4 = me_p // 4
    q = me_p % 4
    u = me_m * 8 + p4
    sib = me_p + 1 - 2 * (me_p % 2)
    xnb = me_p + 2 - 4 * (q // 2)
    q_sib = q + 1 - 2 * (q % 2)
    q_x = q + 2 - 4 * (q // 2)
    q_d = q_sib + 2 - 4 * (q_sib // 2)

    def near_q(quad):
        return ((q // 2 + quad + p4) % 2) * 2 + q % 2

    def near_dp(quad):
        return quad * 4 + near_q(quad)

    def rcopy(src, dst, s, r, dev):
        return pltpu.make_async_remote_copy(
            src_ref=src, dst_ref=dst, send_sem=send.at[s], recv_sem=recv.at[r],
            device_id=dev, device_id_type=MESH)

    load_wi = pltpu.make_async_copy(w_in, wi, wsem.at[0])
    load_wo = pltpu.make_async_copy(w_out, wo, wsem.at[1])
    load_wi.start()
    load_wo.start()

    bar = pltpu.get_barrier_semaphore()

    def sig_row(k, c):
        pl.semaphore_signal(bar, inc=1, device_id=((me_p + k) % NDP, me_m), device_id_type=MESH)
        return c

    lax.fori_loop(1, NDP, sig_row, 0)

    def sig_class(k, c):
        col = (me_m + 1 + k // 8) % NMP
        pl.semaphore_signal(bar, inc=1, device_id=(near_dp(k % 8), col), device_id_type=MESH)
        return c

    lax.fori_loop(0, 56, sig_class, 0)

    r_i = iota((256, 256), 0)
    c_i = iota((256, 256), 1)
    src_row = ((r_i // 2) % 4) * 64 + (r_i // 8) * 2 + r_i % 2
    perm = (c_i == src_row).astype(F32).astype(BF)

    def blocks(ref, out):
        rows = ref[...].reshape(256, 512)
        for h in range(2):
            res = dot(perm, rows[:, h * 256:(h + 1) * 256])
            out[:, h * 8:(h + 1) * 8, :] = res.reshape(32, 8, 256).astype(BF)

    def send_row(src, dst, s, r):
        def body(k, c):
            peer = (me_p + k) % NDP
            rcopy(src.at[peer], dst.at[me_p], s, r, (peer, me_m)).start()
            return c
        lax.fori_loop(1, NDP, body, 0)

    def send_col(src, dst, s, r, spread):
        def body(k, c):
            peer = (me_m + k) % NMP
            part = src.at[peer] if spread else src
            rcopy(part, dst.at[me_m], s, r, (me_p, peer)).start()
            return c
        lax.fori_loop(1, NMP, body, 0)

    blocks(tok, xs)
    pl.semaphore_wait(bar, 31 + 56)
    send_row(xs, xin, S_X, R_X)
    blocks(cot, cs)
    send_row(cs, cin, S_C, R_C)
    xin[me_p] = xs[me_p]
    cin[me_p] = cs[me_p]

    t_i = iota((256, 128), 0)
    l_i = iota((256, 128), 1)
    order = jnp.where(t_i % 2 == 0, grp[0:1, :], grp[1:2, :])
    hit = (order == t_i // 2).astype(F32).astype(BF)
    g_i = iota((8, 128), 0)
    s_i = iota((8, 128), 1)
    pick = (s_i // 32 == g_i % 4).astype(F32).astype(BF)
    own_pos = (iota((8, 256), 1) % 2 == iota((8, 256), 0) // 4).astype(F32)
    m8 = dot_nt(pick, hit) * own_pos

    def half(ref, h, rows):
        return ref[:, h * 8:(h + 1) * 8, :].astype(F32).reshape(rows, ref.shape[-1]).astype(BF)

    wait_bytes(xin.at[pl.ds(0, 31)], recv.at[R_X])
    x0, x1 = half(xin, 0, 256), half(xin, 1, 256)
    r0, r1 = rt[:, 0:256], rt[:, 256:512]
    lsend[...] = (dot_nt(r0, x0) + dot_nt(r1, x1)).reshape(8, 8, 256)
    send_col(lsend, lin, S_L, R_L, True)
    lin[me_m] = lsend[me_m]
    wait_bytes(lin.at[pl.ds(0, 7)], recv.at[R_L])
    logit = jnp.sum(lin[...], axis=0)
    big = jnp.full((8, 256), -jnp.inf, F32)
    peak = jnp.zeros((8, 256), F32)
    for g in range(8):
        inside = jnp.broadcast_to(m8[g:g + 1, :] > 0.5, (8, 256))
        top = jnp.max(jnp.where(inside, logit, big), axis=1, keepdims=True)
        peak = jnp.where(inside, top, peak)
    ex = jnp.exp(logit - peak)
    den = jnp.zeros((8, 256), F32)
    for g in range(8):
        mask = m8[g:g + 1, :]
        den = den + mask * jnp.sum(ex * mask, axis=1, keepdims=True)
    mix_own = ex / den
    mixsend[0:8, :] = mix_own[:, 0:128].astype(BF)
    mixsend[8:16, :] = mix_own[:, 128:256].astype(BF)
    send_col(mixsend, mixall, S_MIX, R_MIX, False)
    mixall[me_m] = mixsend[...]
    wait_bytes(mixall.at[pl.ds(0, 7)], recv.at[R_MIX])

    spread = (iota((512, 64), 0) // 8 == iota((512, 64), 1)).astype(F32).astype(BF)
    for h in range(2):
        wide = dot(spread, half(mixall, h, 64)).reshape(64, 8, 128)
        sel = wide * m8[:, h * 128:(h + 1) * 128][None]
        amat[:, h * 128:(h + 1) * 128] = sel.reshape(512, 128).astype(BF)

    def mixing(rows, buf, dst):
        for h in range(2):
            res = dot(amat[...], rows[h])
            buf[:, h * 8:(h + 1) * 8, :] = res.reshape(64, 8, 256).astype(BF)
        dst[q, u] = buf[u]

    def send_chunk(src, dst, s, r, j):
        def body(k, c):
            m = (me_m + 2 * j + k // 8) % NMP
            quad = (p4 + k) % 8
            rcopy(src.at[m * 8 + quad], dst.at[near_q(quad), u], s, r + j, (near_dp(quad), m)).start()
            return c
        lax.fori_loop(1 if j == 0 else 0, 16, body, 0)

    def chunk_spans(j):
        return [pl.ds(((me_m - 2 * j - i + NMP) % NMP) * 8, 8) for i in range(2)]

    def quad_chunk(g, r_own, s_sib, r_sib, s_x, r_x, j):
        wait_bytes(g.at[0, pl.ds(0, 15 if j == 0 else 16)], recv.at[r_own + j])
        for span in chunk_spans(j):
            part = g.at[q, span]
            rcopy(part, part, s_x, r_x + j, (xnb, me_m)).start()
        for span in chunk_spans(j):
            part = g.at[q, span]
            rcopy(part, part, s_sib, r_sib + j, (sib, me_m)).start()

    def quad_forward(g, r_x, s_f, r_f, j):
        wait_bytes(g.at[0, pl.ds(0, 16)], recv.at[r_x + j])
        for span in chunk_spans(j):
            part = g.at[q_x, span]
            rcopy(part, part, s_f, r_f + j, (sib, me_m)).start()

    def project(g, flat, w, r_sib, r_f, j):
        wait_bytes(g.at[0, pl.ds(0, 16)], recv.at[r_sib + j])
        wait_bytes(g.at[0, pl.ds(0, 16)], recv.at[r_f + j])
        if j == 0:
            acc[...] = jnp.zeros((256, 256), F32)

        def body(i, c):
            m = (me_m - 2 * j - i + NMP) % NMP
            for h in range(2):
                col = pl.multiple_of(m * 512 + h * 256, 256)
                part = g[:, pl.ds(m * 8, 8), h * 8:(h + 1) * 8, :].astype(F32).reshape(256, 256).astype(BF)
                flat[:, pl.ds(col, 256)] = part
                acc[...] += dot_nt(part, w[:, pl.ds(col, 256)])
            return c
        lax.fori_loop(0, 2, body, 0)

    def parts(rows, w, buf, landing, s, r):
        def chunk(j, c):
            jj = (me_m // 2 + j) % CH

            def one(i, c2):
                m = jj * 2 + i
                for h in range(2):
                    col = pl.multiple_of(m * 512 + h * 256, 256)
                    res = dot(rows, w[:, pl.ds(col, 256)])
                    buf[:, pl.ds(m * 8, 8), h * 8:(h + 1) * 8, :] = res.reshape(4, 8, 8, 256).astype(BF)
                return c2
            lax.fori_loop(0, 2, one, 0)
            span = pl.ds(jj * 16, 16)
            rcopy(buf.at[q_d, span], landing.at[1, span], s, r + j, (sib, me_m)).start()
            rcopy(buf.at[q_sib, span], landing.at[0, span], s, r + j, (sib, me_m)).start()
            return c
        lax.fori_loop(0, CH, chunk, 0)

    def pair_sums(buf, landing, out, far, r_sib, s, r):
        def chunk(j, c):
            jj = (me_m // 2 + j) % CH
            span = pl.ds(jj * 16, 16)
            wait_bytes(landing.at[pl.ds(0, 2), span], recv.at[r_sib + j])
            out[span] = (buf[q_x, span].astype(F32) + landing[1, span].astype(F32)).astype(BF)
            rcopy(out.at[span], far.at[span], s, r + j, (xnb, me_m)).start()
            return c
        lax.fori_loop(0, CH, chunk, 0)

    def totals(buf, landing, far, out, home, r_x, s, r):
        def finish(jj, j):
            span = pl.ds(jj * 16, 16)
            wait_bytes(far.at[span], recv.at[r_x + j])
            out[span] = (buf[q, span].astype(F32) + landing[0, span].astype(F32)
                         + far[span].astype(F32)).astype(BF)

        def post(v):
            rcopy(out.at[v], home.at[u], s, r, (near_dp(v % 8), v // 8)).start()

        first = me_m // 2
        finish(first, 0)
        w = u % 16

        def near(k, c):
            post(first * 16 + (w + k) % 16)
            return c
        lax.fori_loop(1, 16, near, 0)
        home[u] = out[u]

        def chunk(j, c):
            jj = (first + j) % CH
            finish(jj, j)

            def each(k, c2):
                post(jj * 16 + (w + k) % 16)
                return c2
            lax.fori_loop(0, 16, each, 0)
            return c
        lax.fori_loop(1, CH, chunk, 0)

    mixing((x0, x1), mbuf, g_fwd)
    for j in range(CH):
        send_chunk(mbuf, g_fwd, S_M, R_M, j)
    wait_bytes(cin.at[pl.ds(0, 31)], recv.at[R_C])
    mixing((half(cin, 0, 256), half(cin, 1, 256)), bbuf, g_back)
    for j in range(CH):
        quad_chunk(g_fwd, R_M, S_QSIB, R_QSIB, S_QX, R_QX, j)
        send_chunk(bbuf, g_back, S_B, R_B, j)
        if j > 0:
            quad_forward(g_fwd, R_QX, S_QF, R_QF, j - 1)
    quad_forward(g_fwd, R_QX, S_QF, R_QF, CH - 1)
    load_wi.wait()
    load_wo.wait()
    for j in range(CH):
        quad_chunk(g_back, R_B, S_BSIB, R_BSIB, S_BX, R_BX, j)
        project(g_fwd, xf, wi, R_QSIB, R_QF, j)
    pre = acc[...]
    sig = 1.0 / (1.0 + jnp.exp(-pre))
    act_f = pre * sig
    slope = sig * (1.0 + pre * (1.0 - sig))
    dtok[:, 0:256] = slope
    active = act_f.astype(BF)
    parts(active, wo, pb, sb, S_PSIB, R_PSIB)
    pair_sums(pb, sb, xsum, xr, R_PSIB, S_PX, R_PX)
    for j in range(CH):
        quad_forward(g_back, R_BX, S_BF, R_BF, j)
    for j in range(CH):
        project(g_back, cf, wo, R_BSIB, R_BF, j)
    d_pre_f = acc[...] * dtok[:, 0:256]
    d_pre = d_pre_f.astype(BF)
    parts(d_pre, wi, pb2, sb2, S_DSIB, R_DSIB)
    pair_sums(pb2, sb2, xsum2, xr2, R_DSIB, S_DX, R_DX)
    totals(pb, sb, xr, rb, pin, R_PX, S_PA, R_PA)
    active_t = act_f.T.astype(BF)
    d_pre_t = d_pre_f.T.astype(BF)

    def weight_grads(m, c):
        col = pl.ds(pl.multiple_of(m * 512, 512), 512)
        go[:, col] = dot(active_t, cf[:, col]).astype(BF)
        gi[:, col] = dot(d_pre_t, xf[:, col]).astype(BF)
        return c
    lax.fori_loop(0, NMP, weight_grads, 0)
    store_wi = pltpu.make_async_copy(gi, o_win, wsem.at[2])
    store_wo = pltpu.make_async_copy(go, o_wout, wsem.at[3])
    store_wi.start()
    store_wo.start()
    totals(pb2, sb2, xr2, rb2, din, R_DX, S_DA, R_DA)

    wait_bytes(pin.at[pl.ds(0, 63)], recv.at[R_PA])
    for h in range(2):
        rows = half(pin, h, 512)
        res = dot_tn(amat[...], rows)
        osend[:, h * 8:(h + 1) * 8, :] = res.reshape(32, 8, 256).astype(BF)
        part = dot_nt(rows, half(cin, h, 256))
        if h == 0:
            bacc[...] = part
        else:
            bacc[...] += part
    send_row(osend, oin, S_O, R_O)
    oin[me_p] = osend[me_p]

    wait_bytes(din.at[pl.ds(0, 63)], recv.at[R_DA])
    for h in range(2):
        bacc[...] += dot_nt(half(din, h, 512), half(xin, h, 256))
    wlsend[...] = jnp.sum(bacc[...].reshape(64, 8, 256) * m8[None], axis=1).reshape(8, 8, 256)
    send_col(wlsend, wlin, S_DW, R_DW, True)
    wlin[me_m] = wlsend[me_m]
    for h in range(2):
        dtok[:, h * 256:(h + 1) * 256] = dot_tn(amat[...], half(din, h, 512))
    wait_bytes(wlin.at[pl.ds(0, 7)], recv.at[R_DW])
    d_weight = jnp.sum(wlin[...], axis=0)
    prod = mix_own * d_weight
    mean = jnp.zeros((8, 256), F32)
    for g in range(8):
        mask = m8[g:g + 1, :]
        mean = mean + mask * jnp.sum(prod * mask, axis=1, keepdims=True)
    d_logit = mix_own * (d_weight - mean)
    dlsend[0:8, :] = d_logit[:, 0:128].astype(BF)
    dlsend[8:16, :] = d_logit[:, 128:256].astype(BF)
    send_col(dlsend, dlall, S_DL, R_DL, False)
    dlall[me_m] = dlsend[...]
    wait_bytes(dlall.at[pl.ds(0, 7)], recv.at[R_DL])
    dl = jnp.concatenate([half(dlall, 0, 64), half(dlall, 1, 64)], axis=1)
    for h in range(2):
        part = dot(dl, half(xin, h, 256))
        for k in range(2):
            tile = part[:, k * 128:(k + 1) * 128].reshape(8, 8, 128)
            for e in range(8):
                rsend[e * 4 + h * 2 + k] = tile[e]
    send_row(rsend, rin, S_R, R_R)
    rin[me_p] = rsend[me_p]
    for h in range(2):
        res = dtok[:, h * 256:(h + 1) * 256] + dot_tn(dl, rt[:, h * 256:(h + 1) * 256])
        gsend[:, h * 8:(h + 1) * 8, :] = res.reshape(32, 8, 256).astype(BF)
    send_row(gsend, gin, S_G, R_G)
    gin[me_p] = gsend[me_p]
    def place(src, out):
        for h in range(2):
            res = dot_tn(perm, half(src, h, 256)).astype(BF)
            out[:, :, h * 256:(h + 1) * 256] = res.reshape(4, 64, 256)

    wait_bytes(oin.at[pl.ds(0, 31)], recv.at[R_O])
    place(oin, o_mix)
    wait_bytes(rin.at[pl.ds(0, 31)], recv.at[R_R])
    rsum[...] = jnp.sum(rin[...], axis=0)

    def share(k, c):
        peer = (me_p + k) % NDP
        rcopy(rsum, rall.at[me_p], S_RG, R_RG, (peer, me_m)).start()
        return c
    lax.fori_loop(1, NDP, share, 0)
    rall[me_p] = rsum[...]

    wait_bytes(gin.at[pl.ds(0, 31)], recv.at[R_G])
    place(gin, o_grad)
    wait_bytes(rall.at[pl.ds(0, 31)], recv.at[R_RG])
    for e in range(8):
        for k in range(4):
            o_router[e * 8:(e + 1) * 8, k * 128:(k + 1) * 128] = rall[e * 4 + k]

    for view, s in (
        (xs.at[pl.ds(0, 31)], S_X), (cs.at[pl.ds(0, 31)], S_C), (lin.at[pl.ds(0, 7)], S_L),
        (mixall.at[pl.ds(0, 7)], S_MIX), (mbuf.at[pl.ds(0, 63)], S_M), (bbuf.at[pl.ds(0, 63)], S_B),
        (g_fwd.at[0], S_QSIB), (g_fwd.at[0], S_QX), (g_fwd.at[0], S_QF),
        (g_back.at[0], S_BSIB), (g_back.at[0], S_BX), (g_back.at[0], S_BF),
        (sb, S_PSIB), (xsum, S_PX), (rb.at[pl.ds(0, 63)], S_PA),
        (sb2, S_DSIB), (xsum2, S_DX), (rb2.at[pl.ds(0, 63)], S_DA),
        (osend.at[pl.ds(0, 31)], S_O), (wlin.at[pl.ds(0, 7)], S_DW), (dlall.at[pl.ds(0, 7)], S_DL),
        (gsend.at[pl.ds(0, 31)], S_G), (rsend.at[pl.ds(0, 31)], S_R), (rall.at[pl.ds(0, 31)], S_RG),
    ):
        wait_bytes(view, send.at[s])
    store_wi.wait()
    store_wo.wait()


def copy_out(*refs):
    count = len(refs) // 2
    sem = refs[-1]
    moves = [pltpu.make_async_copy(refs[i], refs[count + i], sem.at[i]) for i in range(count)]
    for move in moves:
        move.start()
    for move in moves:
        move.wait()


def per_device(tokens, groups, router, w_in, w_out, cotangent):
    vm = lambda shape, dt=BF: pltpu.VMEM(shape, dt)
    blk32, blk64 = (32, 16, 256), (64, 16, 256)
    scratch = [
        vm(blk32), vm(blk32), vm(blk32), vm(blk32),
        vm((8, 8, 256), F32), vm((8, 8, 256), F32), vm((16, 128)), vm((8, 16, 128)), vm((512, 256)),
        vm(blk64), vm(blk64),
        vm((4,) + blk64), vm((4,) + blk64), vm((256, 4096)), vm((256, 4096)),
        vm((256, 4096)), vm((256, 4096)),
        vm((4,) + blk64), vm((2,) + blk64), vm(blk64), vm(blk64), vm(blk64), vm(blk64),
        vm((4,) + blk64), vm((2,) + blk64), vm(blk64), vm(blk64), vm(blk64), vm(blk64),
        vm(blk32), vm(blk32), vm(blk32), vm(blk32),
        vm((8, 8, 256), F32), vm((8, 8, 256), F32), vm((16, 128)), vm((8, 16, 128)), vm((512, 256), F32), vm((256, 512), F32),
        vm((32, 8, 128), F32), vm((32, 8, 128), F32), vm((32, 8, 128), F32), vm((8, 128), F32),
        vm((256, 256), F32), vm((256, 4096)), vm((256, 4096)),
        pltpu.SemaphoreType.DMA((N_SEND,)), pltpu.SemaphoreType.DMA((N_RECV,)),
        pltpu.SemaphoreType.DMA((4,)),
    ]
    in_vmem = pl.BlockSpec(memory_space=pltpu.VMEM)
    anywhere = pl.BlockSpec(memory_space=pl.ANY)
    shapes = (
        jax.ShapeDtypeStruct((4, 64, 512), BF),
        jax.ShapeDtypeStruct((4, 64, 512), BF),
        jax.ShapeDtypeStruct((64, 512), F32),
        jax.ShapeDtypeStruct((256, 4096), BF),
        jax.ShapeDtypeStruct((256, 4096), BF),
    )
    results = pl.pallas_call(
        kernel,
        out_shape=shapes,
        in_specs=[in_vmem, in_vmem, in_vmem, in_vmem, anywhere, anywhere],
        out_specs=[in_vmem, in_vmem, in_vmem, anywhere, anywhere],
        scratch_shapes=scratch,
        compiler_params=pltpu.CompilerParams(
            collective_id=0, has_side_effects=True, vmem_limit_bytes=56 * 1024 * 1024),
        cost_estimate=pl.CostEstimate(flops=4 * 10**9, bytes_accessed=10**7, transcendentals=10**5),
    )(tokens, cotangent, groups, router.T, w_in, w_out)
    mixed_out, tokens_grad, router_t, g_in, g_out = pl.pallas_call(
        copy_out,
        out_shape=shapes,
        in_specs=[anywhere] * 5,
        out_specs=[anywhere] * 5,
        scratch_shapes=[pltpu.SemaphoreType.DMA((5,))],
    )(*results)
    return mixed_out, tokens_grad, router_t.T, g_in, g_out


def solution(mesh):
    return jax.shard_map(
        per_device,
        mesh=mesh,
        in_specs=(
            P("dp", None, "mp"),
            P("dp", None),
            P("mp", None),
            P(("mp", "dp"), None),
            P(("mp", "dp"), None),
            P("dp", None, "mp"),
        ),
        out_specs=(
            P("dp", None, "mp"),
            P("dp", None, "mp"),
            P("mp", None),
            P(("mp", "dp"), None),
            P(("mp", "dp"), None),
        ),
        check_vma=False,
    )
```

```python
import jax
import jax.numpy as jnp
from jax import lax
from jax.experimental import pallas as pl
from jax.experimental.pallas import tpu as pltpu
from jax.sharding import PartitionSpec as P

MESH = pl.DeviceIdType.MESH
BF = jnp.bfloat16
F32 = jnp.float32
NDP = 32
NMP = 8
CH = 4

NT = (((1,), (1,)), ((), ()))
TN = (((0,), (0,)), ((), ()))


def dot(a, b):
    return jnp.dot(a, b, preferred_element_type=F32)


def dot_nt(a, b):
    return lax.dot_general(a, b, NT, preferred_element_type=F32)


def dot_tn(a, b):
    return lax.dot_general(a, b, TN, preferred_element_type=F32)


def iota(shape, dim):
    return lax.broadcasted_iota(jnp.int32, shape, dim)


def wait_bytes(view, sem):
    pltpu.make_async_copy(view, view, sem).wait()


(S_X, S_C, S_L, S_MIX, S_M, S_B, S_QSIB, S_QX, S_QF, S_BSIB, S_BX, S_BF) = range(12)
S_PSIB, S_PX, S_PA, S_DSIB, S_DX, S_DA, S_O, S_DW, S_DL, S_G, S_R, S_RG = range(12, 24)
N_SEND = 24
R_X, R_C, R_L, R_MIX, R_PA, R_DA, R_O, R_DW, R_DL, R_G, R_R, R_RG = range(12)
(R_M, R_B, R_QSIB, R_QX, R_QF, R_BSIB, R_BX, R_BF, R_PSIB, R_PX, R_DSIB, R_DX) = range(12, 60, 4)
N_RECV = 60


def kernel(tok, cot, grp, rt, w_in, w_out,
           o_mix, o_grad, o_router, o_win, o_wout,
           xs, cs, xin, cin, lsend, lin, mixsend, mixall, amat, mbuf, bbuf,
           g_fwd, g_back, xf, cf, wi, wo, pb, sb, xsum, xr, rb, pin,
           pb2, sb2, xsum2, xr2, rb2, din, osend, oin, gsend, gin,
           wlsend, wlin, dlsend, dlall, bacc, dtok, rsend, rin, rall, rsum, acc,
           send, recv, wsem):
    me_p = lax.axis_index("dp")
    me_m = lax.axis_index("mp")
    p4 = me_p // 4
    q = me_p % 4
    u = me_m * 8 + p4
    sib = me_p + 1 - 2 * (me_p % 2)
    xnb = me_p + 2 - 4 * (q // 2)
    q_sib = q + 1 - 2 * (q % 2)
    q_x = q + 2 - 4 * (q // 2)
    q_d = q_sib + 2 - 4 * (q_sib // 2)

    def near_q(quad):
        return ((q // 2 + quad + p4) % 2) * 2 + q % 2

    def near_dp(quad):
        return quad * 4 + near_q(quad)

    def rcopy(src, dst, s, r, dev):
        return pltpu.make_async_remote_copy(
            src_ref=src, dst_ref=dst, send_sem=send.at[s], recv_sem=recv.at[r],
            device_id=dev, device_id_type=MESH)

    load_wi = pltpu.make_async_copy(w_in, wi, wsem.at[0])
    load_wo = pltpu.make_async_copy(w_out, wo, wsem.at[1])
    load_wi.start()
    load_wo.start()

    bar = pltpu.get_barrier_semaphore()

    def sig_row(k, c):
        pl.semaphore_signal(bar, inc=1, device_id=((me_p + k) % NDP, me_m), device_id_type=MESH)
        return c

    lax.fori_loop(1, NDP, sig_row, 0)

    def sig_col(k, c):
        pl.semaphore_signal(bar, inc=1, device_id=(me_p, (me_m + k) % NMP), device_id_type=MESH)
        return c

    lax.fori_loop(1, NMP, sig_col, 0)

    r_i = iota((256, 256), 0)
    c_i = iota((256, 256), 1)
    src_row = ((r_i // 2) % 4) * 64 + (r_i // 8) * 2 + r_i % 2
    perm = (c_i == src_row).astype(F32).astype(BF)

    def blocks(ref, out):
        rows = ref[...].reshape(256, 512)
        for h in range(2):
            res = dot(perm, rows[:, h * 256:(h + 1) * 256])
            out[:, h * 8:(h + 1) * 8, :] = res.reshape(32, 8, 256).astype(BF)

    def send_row(src, dst, s, r):
        def body(k, c):
            peer = (me_p + k) % NDP
            rcopy(src.at[peer], dst.at[me_p], s, r, (peer, me_m)).start()
            return c
        lax.fori_loop(1, NDP, body, 0)

    def send_col(src, dst, s, r, spread):
        def body(k, c):
            peer = (me_m + k) % NMP
            part = src.at[peer] if spread else src
            rcopy(part, dst.at[me_m], s, r, (me_p, peer)).start()
            return c
        lax.fori_loop(1, NMP, body, 0)

    blocks(tok, xs)
    pl.semaphore_wait(bar, 31 + 7)
    send_row(xs, xin, S_X, R_X)
    blocks(cot, cs)
    xin[me_p] = xs[me_p]
    cin[me_p] = cs[me_p]

    t_i = iota((256, 128), 0)
    l_i = iota((256, 128), 1)
    order = jnp.where(t_i % 2 == 0, grp[0:1, :], grp[1:2, :])
    hit = (order == t_i // 2).astype(F32).astype(BF)
    g_i = iota((8, 128), 0)
    s_i = iota((8, 128), 1)
    pick = (s_i // 32 == g_i % 4).astype(F32).astype(BF)
    own_pos = (iota((8, 256), 1) % 2 == iota((8, 256), 0) // 4).astype(F32)
    m8 = dot_nt(pick, hit) * own_pos

    def half(ref, h, rows):
        return ref[:, h * 8:(h + 1) * 8, :].astype(F32).reshape(rows, ref.shape[-1]).astype(BF)

    wait_bytes(xin.at[pl.ds(0, 31)], recv.at[R_X])
    x0, x1 = half(xin, 0, 256), half(xin, 1, 256)
    r0, r1 = rt[:, 0:256], rt[:, 256:512]
    lsend[...] = (dot_nt(r0, x0) + dot_nt(r1, x1)).reshape(8, 8, 256)
    send_col(lsend, lin, S_L, R_L, True)
    send_row(cs, cin, S_C, R_C)
    lin[me_m] = lsend[me_m]
    wait_bytes(lin.at[pl.ds(0, 7)], recv.at[R_L])
    logit = jnp.sum(lin[...], axis=0)
    big = jnp.full((8, 256), -jnp.inf, F32)
    peak = jnp.zeros((8, 256), F32)
    for g in range(8):
        inside = jnp.broadcast_to(m8[g:g + 1, :] > 0.5, (8, 256))
        top = jnp.max(jnp.where(inside, logit, big), axis=1, keepdims=True)
        peak = jnp.where(inside, top, peak)
    ex = jnp.exp(logit - peak)
    den = jnp.zeros((8, 256), F32)
    for g in range(8):
        mask = m8[g:g + 1, :]
        den = den + mask * jnp.sum(ex * mask, axis=1, keepdims=True)
    mix_own = ex / den
    mixsend[0:8, :] = mix_own[:, 0:128].astype(BF)
    mixsend[8:16, :] = mix_own[:, 128:256].astype(BF)
    send_col(mixsend, mixall, S_MIX, R_MIX, False)
    mixall[me_m] = mixsend[...]
    wait_bytes(mixall.at[pl.ds(0, 7)], recv.at[R_MIX])

    spread = (iota((512, 64), 0) // 8 == iota((512, 64), 1)).astype(F32).astype(BF)
    for h in range(2):
        wide = dot(spread, half(mixall, h, 64)).reshape(64, 8, 128)
        sel = wide * m8[:, h * 128:(h + 1) * 128][None]
        amat[:, h * 128:(h + 1) * 128] = sel.reshape(512, 128).astype(BF)

    def mixing(rows, buf, dst):
        for h in range(2):
            res = dot(amat[...], rows[h])
            buf[:, h * 8:(h + 1) * 8, :] = res.reshape(64, 8, 256).astype(BF)
        dst[q, u] = buf[u]

    def send_chunk(src, dst, s, r, j):
        def body(k, c):
            m = (me_m + 2 * j + k // 8) % NMP
            quad = (p4 + k) % 8
            rcopy(src.at[m * 8 + quad], dst.at[near_q(quad), u], s, r + j, (near_dp(quad), m)).start()
            return c
        lax.fori_loop(1 if j == 0 else 0, 16, body, 0)

    def chunk_spans(j):
        return [pl.ds(((me_m - 2 * j - i + NMP) % NMP) * 8, 8) for i in range(2)]

    def quad_chunk(g, r_own, s_sib, r_sib, s_x, r_x, j):
        wait_bytes(g.at[0, pl.ds(0, 15 if j == 0 else 16)], recv.at[r_own + j])
        for span in chunk_spans(j):
            part = g.at[q, span]
            rcopy(part, part, s_x, r_x + j, (xnb, me_m)).start()
        for span in chunk_spans(j):
            part = g.at[q, span]
            rcopy(part, part, s_sib, r_sib + j, (sib, me_m)).start()

    def quad_forward(g, r_x, s_f, r_f, j):
        wait_bytes(g.at[0, pl.ds(0, 16)], recv.at[r_x + j])
        for span in chunk_spans(j):
            part = g.at[q_x, span]
            rcopy(part, part, s_f, r_f + j, (sib, me_m)).start()

    def project(g, flat, w, r_sib, r_f, j):
        wait_bytes(g.at[0, pl.ds(0, 16)], recv.at[r_sib + j])
        wait_bytes(g.at[0, pl.ds(0, 16)], recv.at[r_f + j])
        if j == 0:
            acc[...] = jnp.zeros((256, 256), F32)

        def body(i, c):
            m = (me_m - 2 * j - i + NMP) % NMP
            for h in range(2):
                col = pl.multiple_of(m * 512 + h * 256, 256)
                part = g[:, pl.ds(m * 8, 8), h * 8:(h + 1) * 8, :].astype(F32).reshape(256, 256).astype(BF)
                flat[:, pl.ds(col, 256)] = part
                acc[...] += dot_nt(part, w[:, pl.ds(col, 256)])
            return c
        lax.fori_loop(0, 2, body, 0)

    def parts(rows, w, buf, landing, s, r):
        def chunk(j, c):
            jj = (me_m // 2 + j) % CH

            def one(i, c2):
                m = jj * 2 + i
                for h in range(2):
                    col = pl.multiple_of(m * 512 + h * 256, 256)
                    res = dot(rows, w[:, pl.ds(col, 256)])
                    buf[:, pl.ds(m * 8, 8), h * 8:(h + 1) * 8, :] = res.reshape(4, 8, 8, 256).astype(BF)
                return c2
            lax.fori_loop(0, 2, one, 0)
            span = pl.ds(jj * 16, 16)
            rcopy(buf.at[q_d, span], landing.at[1, span], s, r + j, (sib, me_m)).start()
            rcopy(buf.at[q_sib, span], landing.at[0, span], s, r + j, (sib, me_m)).start()
            return c
        lax.fori_loop(0, CH, chunk, 0)

    def pair_sums(buf, landing, out, far, r_sib, s, r):
        def chunk(j, c):
            jj = (me_m // 2 + j) % CH
            span = pl.ds(jj * 16, 16)
            wait_bytes(landing.at[pl.ds(0, 2), span], recv.at[r_sib + j])
            out[span] = (buf[q_x, span].astype(F32) + landing[1, span].astype(F32)).astype(BF)
            rcopy(out.at[span], far.at[span], s, r + j, (xnb, me_m)).start()
            return c
        lax.fori_loop(0, CH, chunk, 0)

    def total_chunk(buf, landing, far, out, home, r_x, s, r, j):
        jj = (me_m // 2 + j) % CH
        span = pl.ds(jj * 16, 16)
        wait_bytes(far.at[span], recv.at[r_x + j])
        out[span] = (buf[q, span].astype(F32) + landing[0, span].astype(F32)
                     + far[span].astype(F32)).astype(BF)

        def post(k, c):
            v = jj * 16 + (u + k) % 16
            rcopy(out.at[v], home.at[u], s, r, (near_dp(v % 8), v // 8)).start()
            return c
        lax.fori_loop(1 if j == 0 else 0, 16, post, 0)
        if j == 0:
            home[u] = out[u]

    mixing((x0, x1), mbuf, g_fwd)
    for j in range(CH):
        send_chunk(mbuf, g_fwd, S_M, R_M, j)
    wait_bytes(cin.at[pl.ds(0, 31)], recv.at[R_C])
    mixing((half(cin, 0, 256), half(cin, 1, 256)), bbuf, g_back)
    for j in range(CH):
        quad_chunk(g_fwd, R_M, S_QSIB, R_QSIB, S_QX, R_QX, j)
        send_chunk(bbuf, g_back, S_B, R_B, j)
        if j > 0:
            quad_forward(g_fwd, R_QX, S_QF, R_QF, j - 1)
    quad_forward(g_fwd, R_QX, S_QF, R_QF, CH - 1)
    load_wi.wait()
    load_wo.wait()
    for j in range(CH):
        quad_chunk(g_back, R_B, S_BSIB, R_BSIB, S_BX, R_BX, j)
        project(g_fwd, xf, wi, R_QSIB, R_QF, j)
    pre = acc[...]
    sig = 1.0 / (1.0 + jnp.exp(-pre))
    act_f = pre * sig
    slope = sig * (1.0 + pre * (1.0 - sig))
    dtok[:, 0:256] = slope
    active = act_f.astype(BF)
    parts(active, wo, pb, sb, S_PSIB, R_PSIB)
    pair_sums(pb, sb, xsum, xr, R_PSIB, S_PX, R_PX)
    for j in range(CH):
        quad_forward(g_back, R_BX, S_BF, R_BF, j)
    for j in range(CH):
        project(g_back, cf, wo, R_BSIB, R_BF, j)
    d_pre_f = acc[...] * dtok[:, 0:256]
    d_pre = d_pre_f.astype(BF)
    first = (pb, sb, xr, rb, pin, R_PX, S_PA, R_PA)
    second = (pb2, sb2, xr2, rb2, din, R_DX, S_DA, R_DA)
    total_chunk(*first, 0)
    total_chunk(*first, 1)
    parts(d_pre, wi, pb2, sb2, S_DSIB, R_DSIB)
    total_chunk(*first, 2)
    pair_sums(pb2, sb2, xsum2, xr2, R_DSIB, S_DX, R_DX)
    total_chunk(*first, 3)
    active_t = act_f.T.astype(BF)
    d_pre_t = d_pre_f.T.astype(BF)

    def weight_grads(m, c):
        col = pl.ds(pl.multiple_of(m * 512, 512), 512)
        o_wout[:, col] = dot(active_t, cf[:, col]).astype(BF)
        o_win[:, col] = dot(d_pre_t, xf[:, col]).astype(BF)
        return c
    lax.fori_loop(0, NMP, weight_grads, 0)
    for j in range(CH):
        total_chunk(*second, j)

    wait_bytes(pin.at[pl.ds(0, 63)], recv.at[R_PA])
    for h in range(2):
        rows = half(pin, h, 512)
        res = dot_tn(amat[...], rows)
        osend[:, h * 8:(h + 1) * 8, :] = res.reshape(32, 8, 256).astype(BF)
        part = dot_nt(rows, half(cin, h, 256))
        if h == 0:
            bacc[...] = part
        else:
            bacc[...] += part
    send_row(osend, oin, S_O, R_O)
    oin[me_p] = osend[me_p]

    wait_bytes(din.at[pl.ds(0, 63)], recv.at[R_DA])
    for h in range(2):
        bacc[...] += dot_nt(half(din, h, 512), half(xin, h, 256))
    wlsend[...] = jnp.sum(bacc[...].reshape(64, 8, 256) * m8[None], axis=1).reshape(8, 8, 256)
    send_col(wlsend, wlin, S_DW, R_DW, True)
    wlin[me_m] = wlsend[me_m]
    for h in range(2):
        dtok[:, h * 256:(h + 1) * 256] = dot_tn(amat[...], half(din, h, 512))
    wait_bytes(wlin.at[pl.ds(0, 7)], recv.at[R_DW])
    d_weight = jnp.sum(wlin[...], axis=0)
    prod = mix_own * d_weight
    mean = jnp.zeros((8, 256), F32)
    for g in range(8):
        mask = m8[g:g + 1, :]
        mean = mean + mask * jnp.sum(prod * mask, axis=1, keepdims=True)
    d_logit = mix_own * (d_weight - mean)
    dlsend[0:8, :] = d_logit[:, 0:128].astype(BF)
    dlsend[8:16, :] = d_logit[:, 128:256].astype(BF)
    send_col(dlsend, dlall, S_DL, R_DL, False)
    dlall[me_m] = dlsend[...]
    wait_bytes(dlall.at[pl.ds(0, 7)], recv.at[R_DL])
    dl = jnp.concatenate([half(dlall, 0, 64), half(dlall, 1, 64)], axis=1)
    for h in range(2):
        part = dot(dl, half(xin, h, 256))
        for k in range(2):
            tile = part[:, k * 128:(k + 1) * 128].reshape(8, 8, 128)
            for e in range(8):
                rsend[e * 4 + h * 2 + k] = tile[e]
    send_row(rsend, rin, S_R, R_R)
    rin[me_p] = rsend[me_p]
    for h in range(2):
        res = dtok[:, h * 256:(h + 1) * 256] + dot_tn(dl, rt[:, h * 256:(h + 1) * 256])
        gsend[:, h * 8:(h + 1) * 8, :] = res.reshape(32, 8, 256).astype(BF)
    send_row(gsend, gin, S_G, R_G)
    gin[me_p] = gsend[me_p]
    def place(src, out):
        for h in range(2):
            res = dot_tn(perm, half(src, h, 256)).astype(BF)
            out[:, :, h * 256:(h + 1) * 256] = res.reshape(4, 64, 256)

    wait_bytes(oin.at[pl.ds(0, 31)], recv.at[R_O])
    place(oin, o_mix)
    wait_bytes(rin.at[pl.ds(0, 31)], recv.at[R_R])
    rsum[...] = jnp.sum(rin[...], axis=0)

    def share(k, c):
        peer = (me_p + k) % NDP
        rcopy(rsum, rall.at[me_p], S_RG, R_RG, (peer, me_m)).start()
        return c
    lax.fori_loop(1, NDP, share, 0)
    rall[me_p] = rsum[...]

    wait_bytes(gin.at[pl.ds(0, 31)], recv.at[R_G])
    place(gin, o_grad)
    wait_bytes(rall.at[pl.ds(0, 31)], recv.at[R_RG])
    for e in range(8):
        for k in range(4):
            o_router[e * 8:(e + 1) * 8, k * 128:(k + 1) * 128] = rall[e * 4 + k]

    for view, s in (
        (xs.at[pl.ds(0, 31)], S_X), (cs.at[pl.ds(0, 31)], S_C), (lin.at[pl.ds(0, 7)], S_L),
        (mixall.at[pl.ds(0, 7)], S_MIX), (mbuf.at[pl.ds(0, 63)], S_M), (bbuf.at[pl.ds(0, 63)], S_B),
        (g_fwd.at[0], S_QSIB), (g_fwd.at[0], S_QX), (g_fwd.at[0], S_QF),
        (g_back.at[0], S_BSIB), (g_back.at[0], S_BX), (g_back.at[0], S_BF),
        (sb, S_PSIB), (xsum, S_PX), (rb.at[pl.ds(0, 63)], S_PA),
        (sb2, S_DSIB), (xsum2, S_DX), (rb2.at[pl.ds(0, 63)], S_DA),
        (osend.at[pl.ds(0, 31)], S_O), (wlin.at[pl.ds(0, 7)], S_DW), (dlall.at[pl.ds(0, 7)], S_DL),
        (gsend.at[pl.ds(0, 31)], S_G), (rsend.at[pl.ds(0, 31)], S_R), (rall.at[pl.ds(0, 31)], S_RG),
    ):
        wait_bytes(view, send.at[s])


def copy_out(*refs):
    sems = refs[-1]
    moves = [pltpu.make_async_copy(refs[i], refs[5 + i], sems.at[i]) for i in (3, 4, 0, 1, 2)]
    for move in moves:
        move.start()
    for move in moves:
        move.wait()


def per_device(tokens, groups, router, w_in, w_out, cotangent):
    vm = lambda shape, dt=BF: pltpu.VMEM(shape, dt)
    blk32, blk64 = (32, 16, 256), (64, 16, 256)
    scratch = [
        vm(blk32), vm(blk32), vm(blk32), vm(blk32),
        vm((8, 8, 256), F32), vm((8, 8, 256), F32), vm((16, 128)), vm((8, 16, 128)), vm((512, 256)),
        vm(blk64), vm(blk64),
        vm((4,) + blk64), vm((4,) + blk64), vm((256, 4096)), vm((256, 4096)),
        vm((256, 4096)), vm((256, 4096)),
        vm((4,) + blk64), vm((2,) + blk64), vm(blk64), vm(blk64), vm(blk64), vm(blk64),
        vm((4,) + blk64), vm((2,) + blk64), vm(blk64), vm(blk64), vm(blk64), vm(blk64),
        vm(blk32), vm(blk32), vm(blk32), vm(blk32),
        vm((8, 8, 256), F32), vm((8, 8, 256), F32), vm((16, 128)), vm((8, 16, 128)), vm((512, 256), F32), vm((256, 512), F32),
        vm((32, 8, 128), F32), vm((32, 8, 128), F32), vm((32, 8, 128), F32), vm((8, 128), F32),
        vm((256, 256), F32),
        pltpu.SemaphoreType.DMA((N_SEND,)), pltpu.SemaphoreType.DMA((N_RECV,)),
        pltpu.SemaphoreType.DMA((2,)),
    ]
    in_vmem = pl.BlockSpec(memory_space=pltpu.VMEM)
    anywhere = pl.BlockSpec(memory_space=pl.ANY)
    in_hbm = pl.BlockSpec(memory_space=pltpu.HBM)
    shapes = (
        jax.ShapeDtypeStruct((4, 64, 512), BF),
        jax.ShapeDtypeStruct((4, 64, 512), BF),
        jax.ShapeDtypeStruct((64, 512), F32),
        jax.ShapeDtypeStruct((256, 4096), BF),
        jax.ShapeDtypeStruct((256, 4096), BF),
    )
    results = pl.pallas_call(
        kernel,
        out_shape=shapes,
        in_specs=[in_vmem, in_vmem, in_vmem, in_vmem, in_hbm, in_hbm],
        out_specs=[in_vmem] * 5,
        scratch_shapes=scratch,
        compiler_params=pltpu.CompilerParams(
            collective_id=0, has_side_effects=True, vmem_limit_bytes=48 * 1024 * 1024),
        cost_estimate=pl.CostEstimate(flops=4 * 10**9, bytes_accessed=10**7, transcendentals=10**5),
    )(tokens, cotangent, groups, router.T, w_in, w_out)
    mixed_out, tokens_grad, router_t, g_in, g_out = pl.pallas_call(
        copy_out,
        out_shape=shapes,
        in_specs=[anywhere] * 5,
        out_specs=[anywhere] * 5,
        scratch_shapes=[pltpu.SemaphoreType.DMA((5,))],
        compiler_params=pltpu.CompilerParams(vmem_limit_bytes=2 * 1024 * 1024),
    )(*results)
    return mixed_out, tokens_grad, router_t.T, g_in, g_out


def solution(mesh):
    return jax.shard_map(
        per_device,
        mesh=mesh,
        in_specs=(
            P("dp", None, "mp"),
            P("dp", None),
            P("mp", None),
            P(("mp", "dp"), None),
            P(("mp", "dp"), None),
            P("dp", None, "mp"),
        ),
        out_specs=(
            P("dp", None, "mp"),
            P("dp", None, "mp"),
            P("mp", None),
            P(("mp", "dp"), None),
            P(("mp", "dp"), None),
        ),
        check_vma=False,
    )
```

```python
import jax
import jax.numpy as jnp
from jax import lax
from jax.experimental import pallas as pl
from jax.experimental.pallas import tpu as pltpu
from jax.sharding import PartitionSpec as P

MESH = pl.DeviceIdType.MESH
BF = jnp.bfloat16
F32 = jnp.float32
NDP = 32
NMP = 8
CH = 4

NT = (((1,), (1,)), ((), ()))
TN = (((0,), (0,)), ((), ()))


def dot(a, b):
    return jnp.dot(a, b, preferred_element_type=F32)


def dot_nt(a, b):
    return lax.dot_general(a, b, NT, preferred_element_type=F32)


def dot_tn(a, b):
    return lax.dot_general(a, b, TN, preferred_element_type=F32)


def iota(shape, dim):
    return lax.broadcasted_iota(jnp.int32, shape, dim)


def wait_bytes(view, sem):
    pltpu.make_async_copy(view, view, sem).wait()


(S_X, S_C, S_L, S_MIX, S_M, S_B, S_QSIB, S_QX, S_QF, S_BSIB, S_BX, S_BF) = range(12)
S_PSIB, S_PX, S_PA, S_DSIB, S_DX, S_DA, S_O, S_DW, S_DL, S_G, S_R, S_RG, S_T = range(12, 25)
N_SEND = 25
R_X, R_C, R_L, R_MIX, R_PA, R_DA, R_O, R_DW, R_DL, R_G, R_R, R_RG = range(12)
(R_M, R_B, R_QSIB, R_QX, R_QF, R_BSIB, R_BX, R_BF, R_PSIB, R_PX, R_DSIB, R_DX) = range(12, 60, 4)
R_T = 60
N_RECV = 61


def kernel(tok_in, cot_in, grp_in, rt_in, w_in, w_out,
           o_mix, o_grad, o_router, o_win, o_wout,
           tok, cot, grp, rt, xs, cs, xin, cin, lsend, lin, mixsend, mixall, amat, mbuf, bbuf,
           g_fwd, g_back, xf, cf, wi, wo, pb, sb, xsum, xr, rb, pin,
           pb2, sb2, xsum2, xr2, rb2, din, osend, oin, gsend, gin,
           wlsend, wlin, dlsend, dlall, bacc, slope_s, tsend, tin, rsend, rin, rall, rsum, acc,
           send, recv, wsem):
    me_p = lax.axis_index("dp")
    me_m = lax.axis_index("mp")
    p4 = me_p // 4
    q = me_p % 4
    u = me_m * 8 + p4
    sib = me_p + 1 - 2 * (me_p % 2)
    xnb = me_p + 2 - 4 * (q // 2)
    q_sib = q + 1 - 2 * (q % 2)
    q_x = q + 2 - 4 * (q // 2)
    q_d = q_sib + 2 - 4 * (q_sib // 2)

    def near_q(quad):
        return ((q // 2 + quad + p4) % 2) * 2 + q % 2

    def near_dp(quad):
        return quad * 4 + near_q(quad)

    def rcopy(src, dst, s, r, dev):
        return pltpu.make_async_remote_copy(
            src_ref=src, dst_ref=dst, send_sem=send.at[s], recv_sem=recv.at[r],
            device_id=dev, device_id_type=MESH)

    load_wi = pltpu.make_async_copy(w_in, wi, wsem.at[0])
    load_wo = pltpu.make_async_copy(w_out, wo, wsem.at[1])
    load_tok = pltpu.make_async_copy(tok_in, tok, wsem.at[2])
    load_cot = pltpu.make_async_copy(cot_in, cot, wsem.at[3])
    load_grp = pltpu.make_async_copy(grp_in, grp, wsem.at[4])
    load_rt = pltpu.make_async_copy(rt_in, rt, wsem.at[5])
    load_tok.start()
    load_grp.start()
    load_rt.start()
    load_cot.start()

    bar = pltpu.get_barrier_semaphore()

    def sig_row(k, c):
        pl.semaphore_signal(bar, inc=1, device_id=((me_p + k) % NDP, me_m), device_id_type=MESH)
        return c

    lax.fori_loop(1, NDP, sig_row, 0)

    def sig_col(k, c):
        pl.semaphore_signal(bar, inc=1, device_id=(me_p, (me_m + k) % NMP), device_id_type=MESH)
        return c

    lax.fori_loop(1, NMP, sig_col, 0)

    r_i = iota((256, 256), 0)
    c_i = iota((256, 256), 1)
    src_row = ((r_i // 2) % 4) * 64 + (r_i // 8) * 2 + r_i % 2
    perm = (c_i == src_row).astype(F32).astype(BF)

    def blocks(ref, out):
        rows = ref[...].reshape(256, 512)
        for h in range(2):
            res = dot(perm, rows[:, h * 256:(h + 1) * 256])
            out[:, h * 8:(h + 1) * 8, :] = res.reshape(32, 8, 256).astype(BF)

    def send_row(src, dst, s, r):
        def body(k, c):
            peer = (me_p + k) % NDP
            rcopy(src.at[peer], dst.at[me_p], s, r, (peer, me_m)).start()
            return c
        lax.fori_loop(1, NDP, body, 0)

    def send_col(src, dst, s, r, spread):
        def body(k, c):
            peer = (me_m + k) % NMP
            part = src.at[peer] if spread else src
            rcopy(part, dst.at[me_m], s, r, (me_p, peer)).start()
            return c
        lax.fori_loop(1, NMP, body, 0)

    load_tok.wait()
    blocks(tok, xs)
    pl.semaphore_wait(bar, 31 + 7)
    send_row(xs, xin, S_X, R_X)
    load_cot.wait()
    blocks(cot, cs)
    load_wi.start()
    load_wo.start()
    load_grp.wait()
    load_rt.wait()
    xin[me_p] = xs[me_p]
    cin[me_p] = cs[me_p]

    t_i = iota((256, 128), 0)
    l_i = iota((256, 128), 1)
    order = jnp.where(t_i % 2 == 0, grp[0:1, :], grp[1:2, :])
    hit = (order == t_i // 2).astype(F32).astype(BF)
    g_i = iota((8, 128), 0)
    s_i = iota((8, 128), 1)
    pick = (s_i // 32 == g_i % 4).astype(F32).astype(BF)
    own_pos = (iota((8, 256), 1) % 2 == iota((8, 256), 0) // 4).astype(F32)
    m8 = dot_nt(pick, hit) * own_pos

    def half(ref, h, rows):
        return ref[:, h * 8:(h + 1) * 8, :].astype(F32).reshape(rows, ref.shape[-1]).astype(BF)

    wait_bytes(xin.at[pl.ds(0, 31)], recv.at[R_X])
    x0, x1 = half(xin, 0, 256), half(xin, 1, 256)
    r0, r1 = rt[:, 0:256], rt[:, 256:512]
    lsend[...] = (dot_nt(r0, x0) + dot_nt(r1, x1)).reshape(8, 8, 256)
    send_col(lsend, lin, S_L, R_L, True)
    send_row(cs, cin, S_C, R_C)
    lin[me_m] = lsend[me_m]
    wait_bytes(lin.at[pl.ds(0, 7)], recv.at[R_L])
    logit = jnp.sum(lin[...], axis=0)
    big = jnp.full((8, 256), -jnp.inf, F32)
    peak = jnp.zeros((8, 256), F32)
    for g in range(8):
        inside = jnp.broadcast_to(m8[g:g + 1, :] > 0.5, (8, 256))
        top = jnp.max(jnp.where(inside, logit, big), axis=1, keepdims=True)
        peak = jnp.where(inside, top, peak)
    ex = jnp.exp(logit - peak)
    den = jnp.zeros((8, 256), F32)
    for g in range(8):
        mask = m8[g:g + 1, :]
        den = den + mask * jnp.sum(ex * mask, axis=1, keepdims=True)
    mix_own = ex / den
    mixsend[0:8, :] = mix_own[:, 0:128].astype(BF)
    mixsend[8:16, :] = mix_own[:, 128:256].astype(BF)
    send_col(mixsend, mixall, S_MIX, R_MIX, False)
    mixall[me_m] = mixsend[...]
    wait_bytes(mixall.at[pl.ds(0, 7)], recv.at[R_MIX])

    spread = (iota((512, 64), 0) // 8 == iota((512, 64), 1)).astype(F32).astype(BF)
    for h in range(2):
        wide = dot(spread, half(mixall, h, 64)).reshape(64, 8, 128)
        sel = wide * m8[:, h * 128:(h + 1) * 128][None]
        amat[:, h * 128:(h + 1) * 128] = sel.reshape(512, 128).astype(BF)

    def mixing(rows, buf, dst):
        for h in range(2):
            res = dot(amat[...], rows[h])
            buf[:, h * 8:(h + 1) * 8, :] = res.reshape(64, 8, 256).astype(BF)
        dst[q, u] = buf[u]

    def send_chunk(src, dst, s, r, j):
        def body(k, c):
            m = (me_m + 2 * j + k // 8) % NMP
            quad = (p4 + k) % 8
            rcopy(src.at[m * 8 + quad], dst.at[near_q(quad), u], s, r + j, (near_dp(quad), m)).start()
            return c
        lax.fori_loop(1 if j == 0 else 0, 16, body, 0)

    def chunk_spans(j):
        return [pl.ds(((me_m - 2 * j - i + NMP) % NMP) * 8, 8) for i in range(2)]

    def quad_chunk(g, r_own, s_sib, r_sib, s_x, r_x, j):
        wait_bytes(g.at[0, pl.ds(0, 15 if j == 0 else 16)], recv.at[r_own + j])
        for span in chunk_spans(j):
            part = g.at[q, span]
            rcopy(part, part, s_x, r_x + j, (xnb, me_m)).start()
        for span in chunk_spans(j):
            part = g.at[q, span]
            rcopy(part, part, s_sib, r_sib + j, (sib, me_m)).start()

    def quad_forward(g, r_x, s_f, r_f, j):
        wait_bytes(g.at[0, pl.ds(0, 16)], recv.at[r_x + j])
        for span in chunk_spans(j):
            part = g.at[q_x, span]
            rcopy(part, part, s_f, r_f + j, (sib, me_m)).start()

    def project(g, flat, w, r_sib, r_f, j):
        wait_bytes(g.at[0, pl.ds(0, 16)], recv.at[r_sib + j])
        wait_bytes(g.at[0, pl.ds(0, 16)], recv.at[r_f + j])
        if j == 0:
            acc[...] = jnp.zeros((256, 256), F32)

        def body(i, c):
            m = (me_m - 2 * j - i + NMP) % NMP
            for h in range(2):
                col = pl.multiple_of(m * 512 + h * 256, 256)
                part = g[:, pl.ds(m * 8, 8), h * 8:(h + 1) * 8, :].astype(F32).reshape(256, 256).astype(BF)
                flat[:, pl.ds(col, 256)] = part
                acc[...] += dot_nt(part, w[:, pl.ds(col, 256)])
            return c
        lax.fori_loop(0, 2, body, 0)

    def parts(rows, w, buf, landing, s, r):
        def chunk(j, c):
            jj = (me_m // 2 + j) % CH

            def one(i, c2):
                m = jj * 2 + i
                for h in range(2):
                    col = pl.multiple_of(m * 512 + h * 256, 256)
                    res = dot(rows, w[:, pl.ds(col, 256)])
                    buf[:, pl.ds(m * 8, 8), h * 8:(h + 1) * 8, :] = res.reshape(4, 8, 8, 256).astype(BF)
                return c2
            lax.fori_loop(0, 2, one, 0)
            span = pl.ds(jj * 16, 16)
            rcopy(buf.at[q_d, span], landing.at[1, span], s, r + j, (sib, me_m)).start()
            rcopy(buf.at[q_sib, span], landing.at[0, span], s, r + j, (sib, me_m)).start()
            return c
        lax.fori_loop(0, CH, chunk, 0)

    def pair_sums(buf, landing, out, far, r_sib, s, r):
        def chunk(j, c):
            jj = (me_m // 2 + j) % CH
            span = pl.ds(jj * 16, 16)
            wait_bytes(landing.at[pl.ds(0, 2), span], recv.at[r_sib + j])
            out[span] = (buf[q_x, span].astype(F32) + landing[1, span].astype(F32)).astype(BF)
            rcopy(out.at[span], far.at[span], s, r + j, (xnb, me_m)).start()
            return c
        lax.fori_loop(0, CH, chunk, 0)

    def total_chunk(buf, landing, far, out, home, r_x, s, r, j):
        jj = (me_m // 2 + j) % CH
        span = pl.ds(jj * 16, 16)
        wait_bytes(far.at[span], recv.at[r_x + j])
        out[span] = (buf[q, span].astype(F32) + landing[0, span].astype(F32)
                     + far[span].astype(F32)).astype(BF)

        def post(k, c):
            v = jj * 16 + (u + k) % 16
            rcopy(out.at[v], home.at[u], s, r, (near_dp(v % 8), v // 8)).start()
            return c
        lax.fori_loop(1 if j == 0 else 0, 16, post, 0)
        if j == 0:
            home[u] = out[u]

    mixing((x0, x1), mbuf, g_fwd)
    for j in range(CH):
        send_chunk(mbuf, g_fwd, S_M, R_M, j)
    wait_bytes(cin.at[pl.ds(0, 31)], recv.at[R_C])
    mixing((half(cin, 0, 256), half(cin, 1, 256)), bbuf, g_back)
    for j in range(CH):
        quad_chunk(g_fwd, R_M, S_QSIB, R_QSIB, S_QX, R_QX, j)
        send_chunk(bbuf, g_back, S_B, R_B, j)
        if j > 0:
            quad_forward(g_fwd, R_QX, S_QF, R_QF, j - 1)
    quad_forward(g_fwd, R_QX, S_QF, R_QF, CH - 1)
    load_wi.wait()
    load_wo.wait()
    for j in range(CH):
        quad_chunk(g_back, R_B, S_BSIB, R_BSIB, S_BX, R_BX, j)
        project(g_fwd, xf, wi, R_QSIB, R_QF, j)
    pre = acc[...]
    sig = 1.0 / (1.0 + jnp.exp(-pre))
    act_f = pre * sig
    slope = sig * (1.0 + pre * (1.0 - sig))
    slope_s[...] = slope
    active = act_f.astype(BF)
    parts(active, wo, pb, sb, S_PSIB, R_PSIB)
    pair_sums(pb, sb, xsum, xr, R_PSIB, S_PX, R_PX)
    for j in range(CH):
        quad_forward(g_back, R_BX, S_BF, R_BF, j)
    for j in range(CH):
        project(g_back, cf, wo, R_BSIB, R_BF, j)
    d_pre_f = acc[...] * slope_s[...]
    d_pre = d_pre_f.astype(BF)
    first = (pb, sb, xr, rb, pin, R_PX, S_PA, R_PA)
    second = (pb2, sb2, xr2, rb2, din, R_DX, S_DA, R_DA)
    total_chunk(*first, 0)
    total_chunk(*first, 1)
    parts(d_pre, wi, pb2, sb2, S_DSIB, R_DSIB)
    total_chunk(*first, 2)
    pair_sums(pb2, sb2, xsum2, xr2, R_DSIB, S_DX, R_DX)
    total_chunk(*first, 3)
    active_t = act_f.T.astype(BF)
    d_pre_t = d_pre_f.T.astype(BF)

    def weight_grads(m, c):
        col = pl.ds(pl.multiple_of(m * 512, 512), 512)
        o_wout[:, col] = dot(active_t, cf[:, col]).astype(BF)
        o_win[:, col] = dot(d_pre_t, xf[:, col]).astype(BF)
        return c
    lax.fori_loop(0, NMP, weight_grads, 0)
    for j in range(CH):
        total_chunk(*second, j)

    wait_bytes(pin.at[pl.ds(0, 63)], recv.at[R_PA])
    for h in range(2):
        rows = half(pin, h, 512)
        res = dot_tn(amat[...], rows)
        osend[:, h * 8:(h + 1) * 8, :] = res.reshape(32, 8, 256).astype(BF)
        part = dot_nt(rows, half(cin, h, 256))
        if h == 0:
            bacc[...] = part
        else:
            bacc[...] += part
    send_row(osend, oin, S_O, R_O)
    oin[me_p] = osend[me_p]

    wait_bytes(din.at[pl.ds(0, 63)], recv.at[R_DA])
    back_rows = [half(din, h, 512) for h in range(2)]
    for h in range(2):
        bacc[...] += dot_nt(back_rows[h], half(xin, h, 256))
    wlsend[...] = jnp.sum(bacc[...].reshape(64, 8, 256) * m8[None], axis=1).reshape(8, 8, 256)
    send_col(wlsend, wlin, S_DW, R_DW, True)
    wlin[me_m] = wlsend[me_m]
    for h in range(2):
        res = dot_tn(amat[...], back_rows[h])
        gsend[:, h * 8:(h + 1) * 8, :] = res.reshape(32, 8, 256).astype(BF)
    send_row(gsend, gin, S_G, R_G)
    gin[me_p] = gsend[me_p]
    wait_bytes(wlin.at[pl.ds(0, 7)], recv.at[R_DW])
    d_weight = jnp.sum(wlin[...], axis=0)
    prod = mix_own * d_weight
    mean = jnp.zeros((8, 256), F32)
    for g in range(8):
        mask = m8[g:g + 1, :]
        mean = mean + mask * jnp.sum(prod * mask, axis=1, keepdims=True)
    d_logit = mix_own * (d_weight - mean)
    dlsend[0:8, :] = d_logit[:, 0:128].astype(BF)
    dlsend[8:16, :] = d_logit[:, 128:256].astype(BF)
    send_col(dlsend, dlall, S_DL, R_DL, False)
    dlall[me_m] = dlsend[...]
    wait_bytes(dlall.at[pl.ds(0, 7)], recv.at[R_DL])
    dl = jnp.concatenate([half(dlall, 0, 64), half(dlall, 1, 64)], axis=1)
    for h in range(2):
        part = dot(dl, half(xin, h, 256)).astype(BF)
        for e in range(4):
            for k in range(2):
                rsend[e * 4 + h * 2 + k] = part[e * 16:(e + 1) * 16, k * 128:(k + 1) * 128]
    unit = (iota((64, 128), 0) == iota((64, 128), 1)).astype(F32).astype(BF)
    reducer = me_p % 2 == 0
    mine = me_p // 2

    def send_tile(k, c):
        peer = (mine + k) % 16
        rcopy(rsend.at[peer], rin.at[me_p], S_R, R_R, (peer * 2, me_m)).start()
        return c
    lax.fori_loop(1, 16, send_tile, 0)

    @pl.when(me_p % 2 == 1)
    def _():
        rcopy(rsend.at[mine], rin.at[me_p], S_R, R_R, (mine * 2, me_m)).start()

    tsend[...] = dot_tn(dl, unit).reshape(32, 8, 128)
    send_row(tsend, tin, S_T, R_T)
    tin[me_p] = tsend[me_p]

    def place(src, h):
        return dot_tn(perm, half(src, h, 256))

    wait_bytes(oin.at[pl.ds(0, 31)], recv.at[R_O])
    for h in range(2):
        o_mix[:, :, h * 256:(h + 1) * 256] = place(oin, h).reshape(4, 64, 256).astype(BF)

    @pl.when(reducer)
    def _():
        rin[me_p] = rsend[mine]
        wait_bytes(rin.at[pl.ds(0, 31)], recv.at[R_R])
        total = jnp.sum(rin[...].astype(F32), axis=0).astype(BF)
        rsum[...] = total
        rall[mine] = total

        def share(k, c):
            rcopy(rsum, rall.at[mine], S_RG, R_RG, ((me_p + k) % NDP, me_m)).start()
            return c
        lax.fori_loop(1, NDP, share, 0)

    wait_bytes(tin.at[pl.ds(0, 31)], recv.at[R_T])
    d_rows = dot_tn(perm, tin[...].reshape(256, 128).astype(BF)).astype(BF)
    wait_bytes(gin.at[pl.ds(0, 31)], recv.at[R_G])
    for h in range(2):
        cols = slice(h * 256, (h + 1) * 256)
        res = place(gin, h) + dot(d_rows[:, 0:64], rt[:, cols])
        o_grad[:, :, cols] = res.reshape(4, 64, 256).astype(BF)

    @pl.when(reducer)
    def _():
        wait_bytes(rall.at[pl.ds(0, 15)], recv.at[R_RG])

    @pl.when(me_p % 2 == 1)
    def _():
        wait_bytes(rall, recv.at[R_RG])

    for e in range(4):
        for k in range(4):
            o_router[e * 16:(e + 1) * 16, k * 128:(k + 1) * 128] = rall[e * 4 + k].astype(F32)

    @pl.when(me_p % 2 == 1)
    def _():
        wait_bytes(rsend, send.at[S_R])

    @pl.when(reducer)
    def _():
        wait_bytes(rsend.at[pl.ds(0, 15)], send.at[S_R])
        wait_bytes(rin.at[pl.ds(0, 31)], send.at[S_RG])

    for view, s in (
        (xs.at[pl.ds(0, 31)], S_X), (cs.at[pl.ds(0, 31)], S_C), (lin.at[pl.ds(0, 7)], S_L),
        (mixall.at[pl.ds(0, 7)], S_MIX), (mbuf.at[pl.ds(0, 63)], S_M), (bbuf.at[pl.ds(0, 63)], S_B),
        (g_fwd.at[0], S_QSIB), (g_fwd.at[0], S_QX), (g_fwd.at[0], S_QF),
        (g_back.at[0], S_BSIB), (g_back.at[0], S_BX), (g_back.at[0], S_BF),
        (sb, S_PSIB), (xsum, S_PX), (rb.at[pl.ds(0, 63)], S_PA),
        (sb2, S_DSIB), (xsum2, S_DX), (rb2.at[pl.ds(0, 63)], S_DA),
        (osend.at[pl.ds(0, 31)], S_O), (wlin.at[pl.ds(0, 7)], S_DW), (dlall.at[pl.ds(0, 7)], S_DL),
        (gsend.at[pl.ds(0, 31)], S_G), (tsend.at[pl.ds(0, 31)], S_T),
    ):
        wait_bytes(view, send.at[s])


def copy_out(*refs):
    sems = refs[-1]
    moves = [pltpu.make_async_copy(refs[i], refs[5 + i], sems.at[i]) for i in (3, 4, 0, 1, 2)]
    for move in moves:
        move.start()
    for move in moves:
        move.wait()


def per_device(tokens, groups, router, w_in, w_out, cotangent):
    vm = lambda shape, dt=BF: pltpu.VMEM(shape, dt)
    blk32, blk64 = (32, 16, 256), (64, 16, 256)
    scratch = [
        vm((4, 64, 512)), vm((4, 64, 512)), vm((2, 128), jnp.int32), vm((64, 512)),
        vm(blk32), vm(blk32), vm(blk32), vm(blk32),
        vm((8, 8, 256), F32), vm((8, 8, 256), F32), vm((16, 128)), vm((8, 16, 128)), vm((512, 256)),
        vm(blk64), vm(blk64),
        vm((4,) + blk64), vm((4,) + blk64), vm((256, 4096)), vm((256, 4096)),
        vm((256, 4096)), vm((256, 4096)),
        vm((4,) + blk64), vm((2,) + blk64), vm(blk64), vm(blk64), vm(blk64), vm(blk64),
        vm((4,) + blk64), vm((2,) + blk64), vm(blk64), vm(blk64), vm(blk64), vm(blk64),
        vm(blk32), vm(blk32), vm(blk32), vm(blk32),
        vm((8, 8, 256), F32), vm((8, 8, 256), F32), vm((16, 128)), vm((8, 16, 128)), vm((512, 256), F32), vm((256, 256), F32),
        vm((32, 8, 128), F32), vm((32, 8, 128), F32), vm((16, 16, 128)), vm((32, 16, 128)), vm((16, 16, 128)), vm((16, 128)),
        vm((256, 256), F32),
        pltpu.SemaphoreType.DMA((N_SEND,)), pltpu.SemaphoreType.DMA((N_RECV,)),
        pltpu.SemaphoreType.DMA((6,)),
    ]
    in_vmem = pl.BlockSpec(memory_space=pltpu.VMEM)
    anywhere = pl.BlockSpec(memory_space=pl.ANY)
    in_hbm = pl.BlockSpec(memory_space=pltpu.HBM)
    shapes = (
        jax.ShapeDtypeStruct((4, 64, 512), BF),
        jax.ShapeDtypeStruct((4, 64, 512), BF),
        jax.ShapeDtypeStruct((64, 512), F32),
        jax.ShapeDtypeStruct((256, 4096), BF),
        jax.ShapeDtypeStruct((256, 4096), BF),
    )
    results = pl.pallas_call(
        kernel,
        out_shape=shapes,
        in_specs=[in_hbm] * 6,
        out_specs=[in_vmem] * 5,
        scratch_shapes=scratch,
        compiler_params=pltpu.CompilerParams(
            collective_id=0, has_side_effects=True, vmem_limit_bytes=44 * 1024 * 1024),
        cost_estimate=pl.CostEstimate(flops=4 * 10**9, bytes_accessed=10**7, transcendentals=10**5),
    )(*[pltpu.with_memory_space_constraint(a, pltpu.HBM)
        for a in (tokens, cotangent, groups, router.T, w_in, w_out)])
    mixed_out, tokens_grad, router_t, g_in, g_out = pl.pallas_call(
        copy_out,
        out_shape=shapes,
        in_specs=[anywhere] * 5,
        out_specs=[anywhere] * 5,
        scratch_shapes=[pltpu.SemaphoreType.DMA((5,))],
        compiler_params=pltpu.CompilerParams(vmem_limit_bytes=2 * 1024 * 1024),
    )(*results)
    return mixed_out, tokens_grad, router_t.T, g_in, g_out


def solution(mesh):
    return jax.shard_map(
        per_device,
        mesh=mesh,
        in_specs=(
            P("dp", None, "mp"),
            P("dp", None),
            P("mp", None),
            P(("mp", "dp"), None),
            P(("mp", "dp"), None),
            P("dp", None, "mp"),
        ),
        out_specs=(
            P("dp", None, "mp"),
            P("dp", None, "mp"),
            P("mp", None),
            P(("mp", "dp"), None),
            P(("mp", "dp"), None),
        ),
        check_vma=False,
    )
```

```python
import jax
import jax.numpy as jnp
from jax import lax
from jax.experimental import pallas as pl
from jax.experimental.pallas import tpu as pltpu
from jax.sharding import PartitionSpec as P

MESH = pl.DeviceIdType.MESH
BF = jnp.bfloat16
F32 = jnp.float32
NDP = 32
NMP = 8
CH = 8

NT = (((1,), (1,)), ((), ()))
TN = (((0,), (0,)), ((), ()))


def dot(a, b):
    return jnp.dot(a, b, preferred_element_type=F32)


def dot_nt(a, b):
    return lax.dot_general(a, b, NT, preferred_element_type=F32)


def dot_tn(a, b):
    return lax.dot_general(a, b, TN, preferred_element_type=F32)


def iota(shape, dim):
    return lax.broadcasted_iota(jnp.int32, shape, dim)


def wait_bytes(view, sem):
    pltpu.make_async_copy(view, view, sem).wait()


(S_X, S_C, S_L, S_MIX, S_M, S_B, S_QSIB, S_QX, S_QF, S_BSIB, S_BX, S_BF) = range(12)
S_PSIB, S_PX, S_PA, S_DSIB, S_DX, S_DA, S_O, S_DW, S_DL, S_G, S_R, S_RG, S_T = range(12, 25)
N_SEND = 25
R_X, R_C, R_L, R_MIX, R_PA, R_DA, R_O, R_DW, R_DL, R_G, R_R, R_RG = range(12)
(R_M, R_B, R_QSIB, R_QX, R_QF, R_BSIB, R_BX, R_BF, R_PSIB, R_PX, R_DSIB, R_DX) = range(12, 108, 8)
R_T = 108
N_RECV = 109


def kernel(tok_in, cot_in, grp_in, rt_in, w_in, w_out,
           o_mix, o_grad, o_router, o_win, o_wout,
           tok, cot, grp, rt, xs, cs, xin, cin, lsend, lin, mixsend, mixall, amat, mbuf, bbuf,
           g_fwd, g_back, xf, cf, wi, wo, pb, sb, xsum, xr, rb, pin,
           pb2, sb2, xsum2, xr2, rb2, din, osend, oin, gsend, gin,
           wlsend, wlin, dlsend, dlall, bacc, slope_s, tsend, tin, rsend, rin, rall, rsum, acc,
           send, recv, wsem):
    me_p = lax.axis_index("dp")
    me_m = lax.axis_index("mp")
    p4 = me_p // 4
    q = me_p % 4
    u = me_m * 8 + p4
    sib = me_p + 1 - 2 * (me_p % 2)
    xnb = me_p + 2 - 4 * (q // 2)
    q_sib = q + 1 - 2 * (q % 2)
    q_x = q + 2 - 4 * (q // 2)
    q_d = q_sib + 2 - 4 * (q_sib // 2)

    def near_q(quad):
        return ((q // 2 + quad + p4) % 2) * 2 + q % 2

    def near_dp(quad):
        return quad * 4 + near_q(quad)

    def rcopy(src, dst, s, r, dev):
        return pltpu.make_async_remote_copy(
            src_ref=src, dst_ref=dst, send_sem=send.at[s], recv_sem=recv.at[r],
            device_id=dev, device_id_type=MESH)

    load_wi = pltpu.make_async_copy(w_in, wi, wsem.at[0])
    load_wo = pltpu.make_async_copy(w_out, wo, wsem.at[1])
    load_tok = pltpu.make_async_copy(tok_in, tok, wsem.at[2])
    load_cot = pltpu.make_async_copy(cot_in, cot, wsem.at[3])
    load_grp = pltpu.make_async_copy(grp_in, grp, wsem.at[4])
    load_rt = pltpu.make_async_copy(rt_in, rt, wsem.at[5])
    load_tok.start()
    load_grp.start()
    load_rt.start()
    load_cot.start()

    bar = pltpu.get_barrier_semaphore()

    def sig_row(k, c):
        pl.semaphore_signal(bar, inc=1, device_id=((me_p + k) % NDP, me_m), device_id_type=MESH)
        return c

    lax.fori_loop(1, NDP, sig_row, 0)

    def sig_col(k, c):
        pl.semaphore_signal(bar, inc=1, device_id=(me_p, (me_m + k) % NMP), device_id_type=MESH)
        return c

    lax.fori_loop(1, NMP, sig_col, 0)

    r_i = iota((256, 256), 0)
    c_i = iota((256, 256), 1)
    src_row = ((r_i // 2) % 4) * 64 + (r_i // 8) * 2 + r_i % 2
    perm = (c_i == src_row).astype(F32).astype(BF)

    def blocks(ref, out):
        rows = ref[...].reshape(256, 512)
        for h in range(2):
            res = dot(perm, rows[:, h * 256:(h + 1) * 256])
            out[:, h * 8:(h + 1) * 8, :] = res.reshape(32, 8, 256).astype(BF)

    def send_row(src, dst, s, r):
        def body(k, c):
            peer = (me_p + k) % NDP
            rcopy(src.at[peer], dst.at[me_p], s, r, (peer, me_m)).start()
            return c
        lax.fori_loop(1, NDP, body, 0)

    def send_col(src, dst, s, r, spread):
        def body(k, c):
            peer = (me_m + k) % NMP
            part = src.at[peer] if spread else src
            rcopy(part, dst.at[me_m], s, r, (me_p, peer)).start()
            return c
        lax.fori_loop(1, NMP, body, 0)

    load_tok.wait()
    blocks(tok, xs)
    pl.semaphore_wait(bar, 31 + 7)
    send_row(xs, xin, S_X, R_X)
    load_cot.wait()
    blocks(cot, cs)
    load_wi.start()
    load_wo.start()
    load_grp.wait()
    load_rt.wait()
    xin[me_p] = xs[me_p]
    cin[me_p] = cs[me_p]

    t_i = iota((256, 128), 0)
    l_i = iota((256, 128), 1)
    order = jnp.where(t_i % 2 == 0, grp[0:1, :], grp[1:2, :])
    hit = (order == t_i // 2).astype(F32).astype(BF)
    g_i = iota((8, 128), 0)
    s_i = iota((8, 128), 1)
    pick = (s_i // 32 == g_i % 4).astype(F32).astype(BF)
    own_pos = (iota((8, 256), 1) % 2 == iota((8, 256), 0) // 4).astype(F32)
    m8 = dot_nt(pick, hit) * own_pos

    def half(ref, h, rows):
        return ref[:, h * 8:(h + 1) * 8, :].astype(F32).reshape(rows, ref.shape[-1]).astype(BF)

    wait_bytes(xin.at[pl.ds(0, 31)], recv.at[R_X])
    x0, x1 = half(xin, 0, 256), half(xin, 1, 256)
    r0, r1 = rt[:, 0:256], rt[:, 256:512]
    lsend[...] = (dot_nt(r0, x0) + dot_nt(r1, x1)).reshape(8, 8, 256)
    send_col(lsend, lin, S_L, R_L, True)
    send_row(cs, cin, S_C, R_C)
    lin[me_m] = lsend[me_m]
    wait_bytes(lin.at[pl.ds(0, 7)], recv.at[R_L])
    logit = jnp.sum(lin[...], axis=0)
    big = jnp.full((8, 256), -jnp.inf, F32)
    peak = jnp.zeros((8, 256), F32)
    for g in range(8):
        inside = jnp.broadcast_to(m8[g:g + 1, :] > 0.5, (8, 256))
        top = jnp.max(jnp.where(inside, logit, big), axis=1, keepdims=True)
        peak = jnp.where(inside, top, peak)
    ex = jnp.exp(logit - peak)
    den = jnp.zeros((8, 256), F32)
    for g in range(8):
        mask = m8[g:g + 1, :]
        den = den + mask * jnp.sum(ex * mask, axis=1, keepdims=True)
    mix_own = ex / den
    mixsend[0:8, :] = mix_own[:, 0:128].astype(BF)
    mixsend[8:16, :] = mix_own[:, 128:256].astype(BF)
    send_col(mixsend, mixall, S_MIX, R_MIX, False)
    mixall[me_m] = mixsend[...]
    wait_bytes(mixall.at[pl.ds(0, 7)], recv.at[R_MIX])

    spread = (iota((512, 64), 0) // 8 == iota((512, 64), 1)).astype(F32).astype(BF)
    for h in range(2):
        wide = dot(spread, half(mixall, h, 64)).reshape(64, 8, 128)
        sel = wide * m8[:, h * 128:(h + 1) * 128][None]
        amat[:, h * 128:(h + 1) * 128] = sel.reshape(512, 128).astype(BF)

    def mixing(rows, buf, dst):
        for h in range(2):
            res = dot(amat[...], rows[h])
            buf[:, h * 8:(h + 1) * 8, :] = res.reshape(64, 8, 256).astype(BF)
        dst[q, u] = buf[u]

    def send_chunk(src, dst, s, r, j):
        m = (me_m + j) % NMP

        def body(k, c):
            quad = (p4 + k) % 8
            rcopy(src.at[m * 8 + quad], dst.at[near_q(quad), u], s, r + j, (near_dp(quad), m)).start()
            return c
        lax.fori_loop(1 if j == 0 else 0, 8, body, 0)

    def chunk_span(j):
        return pl.ds(((me_m - j + NMP) % NMP) * 8, 8)

    def quad_chunk(g, r_own, s_sib, r_sib, s_x, r_x, j):
        wait_bytes(g.at[0, pl.ds(0, 7 if j == 0 else 8)], recv.at[r_own + j])
        part = g.at[q, chunk_span(j)]
        rcopy(part, part, s_x, r_x + j, (xnb, me_m)).start()
        rcopy(part, part, s_sib, r_sib + j, (sib, me_m)).start()

    def quad_forward(g, r_x, s_f, r_f, j):
        part = g.at[q_x, chunk_span(j)]
        wait_bytes(part, recv.at[r_x + j])
        rcopy(part, part, s_f, r_f + j, (sib, me_m)).start()

    def project(g, flat, w, r_sib, r_f, j):
        m = (me_m - j + NMP) % NMP
        wait_bytes(g.at[0, pl.ds(0, 8)], recv.at[r_sib + j])
        wait_bytes(g.at[0, pl.ds(0, 8)], recv.at[r_f + j])
        for h in range(2):
            col = pl.multiple_of(m * 512 + h * 256, 256)
            part = g[:, pl.ds(m * 8, 8), h * 8:(h + 1) * 8, :].astype(F32).reshape(256, 256).astype(BF)
            flat[:, pl.ds(col, 256)] = part
            res = dot_nt(part, w[:, pl.ds(col, 256)])
            if j == 0 and h == 0:
                acc[...] = res
            else:
                acc[...] += res

    def parts(rows, w, buf, landing, s, r):
        def chunk(j, c):
            m = (me_m + j) % NMP
            for h in range(2):
                col = pl.multiple_of(m * 512 + h * 256, 256)
                res = dot(rows, w[:, pl.ds(col, 256)])
                buf[:, pl.ds(m * 8, 8), h * 8:(h + 1) * 8, :] = res.reshape(4, 8, 8, 256).astype(BF)
            span = pl.ds(m * 8, 8)
            rcopy(buf.at[q_d, span], landing.at[1, span], s, r + j, (sib, me_m)).start()
            rcopy(buf.at[q_sib, span], landing.at[0, span], s, r + j, (sib, me_m)).start()
            return c
        lax.fori_loop(0, CH, chunk, 0)

    def pair_sum(buf, landing, out, far, r_sib, s, r, j):
        span = pl.ds(((me_m + j) % NMP) * 8, 8)
        wait_bytes(landing.at[pl.ds(0, 2), span], recv.at[r_sib + j])
        out[span] = (buf[q_x, span].astype(F32) + landing[1, span].astype(F32)).astype(BF)
        rcopy(out.at[span], far.at[span], s, r + j, (xnb, me_m)).start()

    def total_chunk(buf, landing, far, out, home, r_x, s, r, j):
        m = (me_m + j) % NMP
        span = pl.ds(m * 8, 8)
        wait_bytes(far.at[span], recv.at[r_x + j])
        out[span] = (buf[q, span].astype(F32) + landing[0, span].astype(F32)
                     + far[span].astype(F32)).astype(BF)

        def post(k, c):
            quad = (p4 + k) % 8
            rcopy(out.at[m * 8 + quad], home.at[u], s, r, (near_dp(quad), m)).start()
            return c
        lax.fori_loop(1 if j == 0 else 0, 8, post, 0)
        if j == 0:
            home[u] = out[u]

    mixing((x0, x1), mbuf, g_fwd)
    for j in range(CH):
        send_chunk(mbuf, g_fwd, S_M, R_M, j)
    wait_bytes(cin.at[pl.ds(0, 31)], recv.at[R_C])
    mixing((half(cin, 0, 256), half(cin, 1, 256)), bbuf, g_back)
    for j in range(CH):
        quad_chunk(g_fwd, R_M, S_QSIB, R_QSIB, S_QX, R_QX, j)
        send_chunk(bbuf, g_back, S_B, R_B, j)
        if j > 0:
            quad_forward(g_fwd, R_QX, S_QF, R_QF, j - 1)
    quad_forward(g_fwd, R_QX, S_QF, R_QF, CH - 1)
    load_wi.wait()
    load_wo.wait()
    for j in range(CH):
        project(g_fwd, xf, wi, R_QSIB, R_QF, j)
    pre = acc[...]
    sig = 1.0 / (1.0 + jnp.exp(-pre))
    act_f = pre * sig
    slope_s[...] = sig * (1.0 + pre * (1.0 - sig))
    active = act_f.astype(BF)
    active_t = act_f.T.astype(BF)
    parts(active, wo, pb, sb, S_PSIB, R_PSIB)
    first = (pb, sb, xr, rb, pin, R_PX, S_PA, R_PA)
    second = (pb2, sb2, xr2, rb2, din, R_DX, S_DA, R_DA)
    for j in range(CH):
        quad_chunk(g_back, R_B, S_BSIB, R_BSIB, S_BX, R_BX, j)
        pair_sum(pb, sb, xsum, xr, R_PSIB, S_PX, R_PX, j)
        if j > 0:
            quad_forward(g_back, R_BX, S_BF, R_BF, j - 1)
            total_chunk(*first, j - 1)
            project(g_back, cf, wo, R_BSIB, R_BF, j - 1)
    quad_forward(g_back, R_BX, S_BF, R_BF, CH - 1)
    project(g_back, cf, wo, R_BSIB, R_BF, CH - 1)
    d_pre_f = acc[...] * slope_s[...]
    d_pre = d_pre_f.astype(BF)
    parts(d_pre, wi, pb2, sb2, S_DSIB, R_DSIB)
    for j in range(CH):
        pair_sum(pb2, sb2, xsum2, xr2, R_DSIB, S_DX, R_DX, j)
    total_chunk(*first, CH - 1)
    d_pre_t = d_pre_f.T.astype(BF)

    def weight_grad(out, lhs, rhs):
        def body(m, c):
            col = pl.ds(pl.multiple_of(m * 512, 512), 512)
            out[:, col] = dot(lhs, rhs[:, col]).astype(BF)
            return c
        lax.fori_loop(0, NMP, body, 0)

    weight_grad(o_wout, active_t, cf)
    for j in range(CH):
        total_chunk(*second, j)

    wait_bytes(pin.at[pl.ds(0, 63)], recv.at[R_PA])
    for h in range(2):
        rows = half(pin, h, 512)
        res = dot_tn(amat[...], rows)
        osend[:, h * 8:(h + 1) * 8, :] = res.reshape(32, 8, 256).astype(BF)
        part = dot_nt(rows, half(cin, h, 256))
        if h == 0:
            bacc[...] = part
        else:
            bacc[...] += part
    send_row(osend, oin, S_O, R_O)
    oin[me_p] = osend[me_p]

    weight_grad(o_win, d_pre_t, xf)

    wait_bytes(din.at[pl.ds(0, 63)], recv.at[R_DA])
    back_rows = [half(din, h, 512) for h in range(2)]
    for h in range(2):
        bacc[...] += dot_nt(back_rows[h], half(xin, h, 256))
    wlsend[...] = jnp.sum(bacc[...].reshape(64, 8, 256) * m8[None], axis=1).reshape(8, 8, 256)
    send_col(wlsend, wlin, S_DW, R_DW, True)
    wlin[me_m] = wlsend[me_m]
    for h in range(2):
        res = dot_tn(amat[...], back_rows[h])
        gsend[:, h * 8:(h + 1) * 8, :] = res.reshape(32, 8, 256).astype(BF)
    send_row(gsend, gin, S_G, R_G)
    gin[me_p] = gsend[me_p]
    wait_bytes(wlin.at[pl.ds(0, 7)], recv.at[R_DW])
    d_weight = jnp.sum(wlin[...], axis=0)
    prod = mix_own * d_weight
    mean = jnp.zeros((8, 256), F32)
    for g in range(8):
        mask = m8[g:g + 1, :]
        mean = mean + mask * jnp.sum(prod * mask, axis=1, keepdims=True)
    d_logit = mix_own * (d_weight - mean)
    dlsend[0:8, :] = d_logit[:, 0:128].astype(BF)
    dlsend[8:16, :] = d_logit[:, 128:256].astype(BF)
    send_col(dlsend, dlall, S_DL, R_DL, False)
    dlall[me_m] = dlsend[...]
    wait_bytes(dlall.at[pl.ds(0, 7)], recv.at[R_DL])
    dl = jnp.concatenate([half(dlall, 0, 64), half(dlall, 1, 64)], axis=1)
    for h in range(2):
        part = dot(dl, half(xin, h, 256)).astype(BF)
        for e in range(4):
            for k in range(2):
                rsend[e * 4 + h * 2 + k] = part[e * 16:(e + 1) * 16, k * 128:(k + 1) * 128]
    unit = (iota((64, 128), 0) == iota((64, 128), 1)).astype(F32).astype(BF)
    reducer = me_p % 2 == 0
    mine = me_p // 2

    def send_tile(k, c):
        peer = (mine + k) % 16
        rcopy(rsend.at[peer], rin.at[me_p], S_R, R_R, (peer * 2, me_m)).start()
        return c
    lax.fori_loop(1, 16, send_tile, 0)

    @pl.when(me_p % 2 == 1)
    def _():
        rcopy(rsend.at[mine], rin.at[me_p], S_R, R_R, (mine * 2, me_m)).start()

    tsend[...] = dot_tn(dl, unit).reshape(32, 8, 128)
    send_row(tsend, tin, S_T, R_T)
    tin[me_p] = tsend[me_p]

    def place(src, h):
        return dot_tn(perm, half(src, h, 256))

    wait_bytes(oin.at[pl.ds(0, 31)], recv.at[R_O])
    for h in range(2):
        o_mix[:, :, h * 256:(h + 1) * 256] = place(oin, h).reshape(4, 64, 256).astype(BF)

    @pl.when(reducer)
    def _():
        rin[me_p] = rsend[mine]
        wait_bytes(rin.at[pl.ds(0, 31)], recv.at[R_R])
        total = jnp.sum(rin[...].astype(F32), axis=0).astype(BF)
        rsum[...] = total
        rall[mine] = total

        def share(k, c):
            rcopy(rsum, rall.at[mine], S_RG, R_RG, ((me_p + k) % NDP, me_m)).start()
            return c
        lax.fori_loop(1, NDP, share, 0)

    wait_bytes(tin.at[pl.ds(0, 31)], recv.at[R_T])
    d_rows = dot_tn(perm, tin[...].reshape(256, 128).astype(BF)).astype(BF)
    wait_bytes(gin.at[pl.ds(0, 31)], recv.at[R_G])
    for h in range(2):
        cols = slice(h * 256, (h + 1) * 256)
        res = place(gin, h) + dot(d_rows[:, 0:64], rt[:, cols])
        o_grad[:, :, cols] = res.reshape(4, 64, 256).astype(BF)

    @pl.when(reducer)
    def _():
        wait_bytes(rall.at[pl.ds(0, 15)], recv.at[R_RG])

    @pl.when(me_p % 2 == 1)
    def _():
        wait_bytes(rall, recv.at[R_RG])

    for e in range(4):
        for k in range(4):
            o_router[e * 16:(e + 1) * 16, k * 128:(k + 1) * 128] = rall[e * 4 + k].astype(F32)

    @pl.when(me_p % 2 == 1)
    def _():
        wait_bytes(rsend, send.at[S_R])

    @pl.when(reducer)
    def _():
        wait_bytes(rsend.at[pl.ds(0, 15)], send.at[S_R])
        wait_bytes(rin.at[pl.ds(0, 31)], send.at[S_RG])

    for view, s in (
        (xs.at[pl.ds(0, 31)], S_X), (cs.at[pl.ds(0, 31)], S_C), (lin.at[pl.ds(0, 7)], S_L),
        (mixall.at[pl.ds(0, 7)], S_MIX), (mbuf.at[pl.ds(0, 63)], S_M), (bbuf.at[pl.ds(0, 63)], S_B),
        (g_fwd.at[0], S_QSIB), (g_fwd.at[0], S_QX), (g_fwd.at[0], S_QF),
        (g_back.at[0], S_BSIB), (g_back.at[0], S_BX), (g_back.at[0], S_BF),
        (sb, S_PSIB), (xsum, S_PX), (rb.at[pl.ds(0, 63)], S_PA),
        (sb2, S_DSIB), (xsum2, S_DX), (rb2.at[pl.ds(0, 63)], S_DA),
        (osend.at[pl.ds(0, 31)], S_O), (wlin.at[pl.ds(0, 7)], S_DW), (dlall.at[pl.ds(0, 7)], S_DL),
        (gsend.at[pl.ds(0, 31)], S_G), (tsend.at[pl.ds(0, 31)], S_T),
    ):
        wait_bytes(view, send.at[s])


def copy_out(*refs):
    sems = refs[-1]
    moves = [pltpu.make_async_copy(refs[i], refs[5 + i], sems.at[i]) for i in (3, 4, 0, 1, 2)]
    for move in moves:
        move.start()
    for move in moves:
        move.wait()


def per_device(tokens, groups, router, w_in, w_out, cotangent):
    vm = lambda shape, dt=BF: pltpu.VMEM(shape, dt)
    blk32, blk64 = (32, 16, 256), (64, 16, 256)
    scratch = [
        vm((4, 64, 512)), vm((4, 64, 512)), vm((2, 128), jnp.int32), vm((64, 512)),
        vm(blk32), vm(blk32), vm(blk32), vm(blk32),
        vm((8, 8, 256), F32), vm((8, 8, 256), F32), vm((16, 128)), vm((8, 16, 128)), vm((512, 256)),
        vm(blk64), vm(blk64),
        vm((4,) + blk64), vm((4,) + blk64), vm((256, 4096)), vm((256, 4096)),
        vm((256, 4096)), vm((256, 4096)),
        vm((4,) + blk64), vm((2,) + blk64), vm(blk64), vm(blk64), vm(blk64), vm(blk64),
        vm((4,) + blk64), vm((2,) + blk64), vm(blk64), vm(blk64), vm(blk64), vm(blk64),
        vm(blk32), vm(blk32), vm(blk32), vm(blk32),
        vm((8, 8, 256), F32), vm((8, 8, 256), F32), vm((16, 128)), vm((8, 16, 128)), vm((512, 256), F32), vm((256, 256), F32),
        vm((32, 8, 128), F32), vm((32, 8, 128), F32), vm((16, 16, 128)), vm((32, 16, 128)), vm((16, 16, 128)), vm((16, 128)),
        vm((256, 256), F32),
        pltpu.SemaphoreType.DMA((N_SEND,)), pltpu.SemaphoreType.DMA((N_RECV,)),
        pltpu.SemaphoreType.DMA((6,)),
    ]
    in_vmem = pl.BlockSpec(memory_space=pltpu.VMEM)
    anywhere = pl.BlockSpec(memory_space=pl.ANY)
    in_hbm = pl.BlockSpec(memory_space=pltpu.HBM)
    shapes = (
        jax.ShapeDtypeStruct((4, 64, 512), BF),
        jax.ShapeDtypeStruct((4, 64, 512), BF),
        jax.ShapeDtypeStruct((64, 512), F32),
        jax.ShapeDtypeStruct((256, 4096), BF),
        jax.ShapeDtypeStruct((256, 4096), BF),
    )
    results = pl.pallas_call(
        kernel,
        out_shape=shapes,
        in_specs=[in_hbm] * 6,
        out_specs=[in_vmem] * 5,
        scratch_shapes=scratch,
        compiler_params=pltpu.CompilerParams(
            collective_id=0, has_side_effects=True, vmem_limit_bytes=44 * 1024 * 1024),
        cost_estimate=pl.CostEstimate(flops=4 * 10**9, bytes_accessed=10**7, transcendentals=10**5),
    )(*[pltpu.with_memory_space_constraint(a, pltpu.HBM)
        for a in (tokens, cotangent, groups, router.T, w_in, w_out)])
    mixed_out, tokens_grad, router_t, g_in, g_out = pl.pallas_call(
        copy_out,
        out_shape=shapes,
        in_specs=[anywhere] * 5,
        out_specs=[anywhere] * 5,
        scratch_shapes=[pltpu.SemaphoreType.DMA((5,))],
        compiler_params=pltpu.CompilerParams(vmem_limit_bytes=2 * 1024 * 1024),
    )(*results)
    return mixed_out, tokens_grad, router_t.T, g_in, g_out


def solution(mesh):
    return jax.shard_map(
        per_device,
        mesh=mesh,
        in_specs=(
            P("dp", None, "mp"),
            P("dp", None),
            P("mp", None),
            P(("mp", "dp"), None),
            P(("mp", "dp"), None),
            P("dp", None, "mp"),
        ),
        out_specs=(
            P("dp", None, "mp"),
            P("dp", None, "mp"),
            P("mp", None),
            P(("mp", "dp"), None),
            P(("mp", "dp"), None),
        ),
        check_vma=False,
    )
```

```python
import jax
import jax.numpy as jnp
from jax import lax
from jax.experimental import pallas as pl
from jax.experimental.pallas import tpu as pltpu
from jax.sharding import PartitionSpec as P

MESH = pl.DeviceIdType.MESH
BF = jnp.bfloat16
F32 = jnp.float32
NDP = 32
NMP = 8
CH = 8

NT = (((1,), (1,)), ((), ()))
TN = (((0,), (0,)), ((), ()))


def dot(a, b):
    return jnp.dot(a, b, preferred_element_type=F32)


def dot_nt(a, b):
    return lax.dot_general(a, b, NT, preferred_element_type=F32)


def dot_tn(a, b):
    return lax.dot_general(a, b, TN, preferred_element_type=F32)


def iota(shape, dim):
    return lax.broadcasted_iota(jnp.int32, shape, dim)


def wait_bytes(view, sem):
    pltpu.make_async_copy(view, view, sem).wait()


(S_X, S_C, S_L, S_MIX, S_M, S_B, S_QSIB, S_QX, S_QF, S_BSIB, S_BX, S_BF) = range(12)
S_PSIB, S_PX, S_PA, S_DSIB, S_DX, S_DA, S_O, S_DW, S_DL, S_G, S_R, S_RG = range(12, 24)
N_SEND = 24
R_X, R_C, R_L, R_MIX, R_PA, R_DA, R_O, R_DW, R_DL, R_G, R_R, R_RG = range(12)
(R_M, R_B, R_QSIB, R_QX, R_QF, R_BSIB, R_BX, R_BF, R_PSIB, R_PX, R_DSIB, R_DX) = range(12, 108, 8)
N_RECV = 108


def kernel(tok_in, cot_in, grp_in, rt_in, w_in, w_out,
           o_mix, o_grad, o_router, o_win, o_wout,
           tok, cot, grp, rt, xs, cs, xin, cin, lsend, lin, mixsend, mixall, amat, mbuf, bbuf,
           g_fwd, g_back, xf, cf, wi, wo, pb, sb, xsum, xr, rb, pin,
           pb2, sb2, xsum2, xr2, rb2, din, osend, oin, gsend, gin,
           wlsend, wlin, dlsend, dlall, bacc, slope_s, rows_s, rows2_s, lhs_s, lhs2_s, rsend, rin, rall, rsum, acc,
           send, recv, wsem):
    me_p = lax.axis_index("dp")
    me_m = lax.axis_index("mp")
    p4 = me_p // 4
    q = me_p % 4
    u = me_m * 8 + p4
    sib = me_p + 1 - 2 * (me_p % 2)
    xnb = me_p + 2 - 4 * (q // 2)
    q_sib = q + 1 - 2 * (q % 2)
    q_x = q + 2 - 4 * (q // 2)
    q_d = q_sib + 2 - 4 * (q_sib // 2)

    def near_q(quad):
        return ((q // 2 + quad + p4) % 2) * 2 + q % 2

    def near_dp(quad):
        return quad * 4 + near_q(quad)

    def rcopy(src, dst, s, r, dev):
        return pltpu.make_async_remote_copy(
            src_ref=src, dst_ref=dst, send_sem=send.at[s], recv_sem=recv.at[r],
            device_id=dev, device_id_type=MESH)

    load_wi = pltpu.make_async_copy(w_in, wi, wsem.at[0])
    load_wo = pltpu.make_async_copy(w_out, wo, wsem.at[1])
    load_tok = pltpu.make_async_copy(tok_in, tok, wsem.at[2])
    load_cot = pltpu.make_async_copy(cot_in, cot, wsem.at[3])
    load_grp = pltpu.make_async_copy(grp_in, grp, wsem.at[4])
    load_rt = pltpu.make_async_copy(rt_in, rt, wsem.at[5])
    load_tok.start()
    load_grp.start()
    load_rt.start()
    load_cot.start()

    bar = pltpu.get_barrier_semaphore()

    def sig_row(k, c):
        pl.semaphore_signal(bar, inc=1, device_id=((me_p + k) % NDP, me_m), device_id_type=MESH)
        return c

    lax.fori_loop(1, NDP, sig_row, 0)

    def sig_col(k, c):
        pl.semaphore_signal(bar, inc=1, device_id=(me_p, (me_m + k) % NMP), device_id_type=MESH)
        return c

    lax.fori_loop(1, NMP, sig_col, 0)

    r_i = iota((256, 256), 0)
    c_i = iota((256, 256), 1)
    src_row = ((r_i // 2) % 4) * 64 + (r_i // 8) * 2 + r_i % 2
    perm = (c_i == src_row).astype(F32).astype(BF)

    def blocks(ref, out):
        rows = ref[...].reshape(256, 512)
        for h in range(2):
            res = dot(perm, rows[:, h * 256:(h + 1) * 256])
            out[:, h * 8:(h + 1) * 8, :] = res.reshape(32, 8, 256).astype(BF)

    def send_row(src, dst, s, r, low=1, high=NDP):
        def body(k, c):
            peer = (me_p + k) % NDP
            rcopy(src.at[peer], dst.at[me_p], s, r, (peer, me_m)).start()
            return c
        lax.fori_loop(low, high, body, 0)

    def send_col(src, dst, s, r, spread):
        def body(k, c):
            peer = (me_m + k) % NMP
            part = src.at[peer] if spread else src
            rcopy(part, dst.at[me_m], s, r, (me_p, peer)).start()
            return c
        lax.fori_loop(1, NMP, body, 0)

    load_tok.wait()
    blocks(tok, xs)
    pl.semaphore_wait(bar, 31 + 7)
    send_row(xs, xin, S_X, R_X)
    load_cot.wait()
    blocks(cot, cs)
    send_row(cs, cin, S_C, R_C)
    load_wi.start()
    load_wo.start()
    load_grp.wait()
    load_rt.wait()
    xin[me_p] = xs[me_p]
    cin[me_p] = cs[me_p]

    t_i = iota((256, 128), 0)
    l_i = iota((256, 128), 1)
    order = jnp.where(t_i % 2 == 0, grp[0:1, :], grp[1:2, :])
    hit = (order == t_i // 2).astype(F32).astype(BF)
    g_i = iota((8, 128), 0)
    s_i = iota((8, 128), 1)
    pick = (s_i // 32 == g_i % 4).astype(F32).astype(BF)
    own_pos = (iota((8, 256), 1) % 2 == iota((8, 256), 0) // 4).astype(F32)
    m8 = dot_nt(pick, hit) * own_pos

    def half(ref, h, rows):
        return ref[:, h * 8:(h + 1) * 8, :].astype(F32).reshape(rows, ref.shape[-1]).astype(BF)

    wait_bytes(xin.at[pl.ds(0, 31)], recv.at[R_X])
    x0, x1 = half(xin, 0, 256), half(xin, 1, 256)
    r0, r1 = rt[:, 0:256], rt[:, 256:512]
    lsend[...] = (dot_nt(r0, x0) + dot_nt(r1, x1)).reshape(8, 8, 256)
    send_col(lsend, lin, S_L, R_L, True)
    lin[me_m] = lsend[me_m]
    wait_bytes(lin.at[pl.ds(0, 7)], recv.at[R_L])
    logit = jnp.sum(lin[...], axis=0)
    big = jnp.full((8, 256), -jnp.inf, F32)
    peak = jnp.zeros((8, 256), F32)
    for g in range(8):
        inside = jnp.broadcast_to(m8[g:g + 1, :] > 0.5, (8, 256))
        top = jnp.max(jnp.where(inside, logit, big), axis=1, keepdims=True)
        peak = jnp.where(inside, top, peak)
    ex = jnp.exp(logit - peak)
    den = jnp.zeros((8, 256), F32)
    for g in range(8):
        mask = m8[g:g + 1, :]
        den = den + mask * jnp.sum(ex * mask, axis=1, keepdims=True)
    mix_own = ex / den
    mixsend[0:8, :] = mix_own[:, 0:128].astype(BF)
    mixsend[8:16, :] = mix_own[:, 128:256].astype(BF)
    send_col(mixsend, mixall, S_MIX, R_MIX, False)
    mixall[me_m] = mixsend[...]
    wait_bytes(mixall.at[pl.ds(0, 7)], recv.at[R_MIX])

    spread = (iota((512, 64), 0) // 8 == iota((512, 64), 1)).astype(F32).astype(BF)
    for h in range(2):
        wide = dot(spread, half(mixall, h, 64)).reshape(64, 8, 128)
        sel = wide * m8[:, h * 128:(h + 1) * 128][None]
        amat[:, h * 128:(h + 1) * 128] = sel.reshape(512, 128).astype(BF)

    def mixing(rows, buf, dst):
        for h in range(2):
            res = dot(amat[...], rows[h])
            buf[:, h * 8:(h + 1) * 8, :] = res.reshape(64, 8, 256).astype(BF)
        dst[q, u] = buf[u]

    def send_chunk(src, dst, s, r, j):
        m = (me_m + j) % NMP

        def body(k, c):
            quad = (p4 + k) % 8
            rcopy(src.at[m * 8 + quad], dst.at[near_q(quad), u], s, r + j, (near_dp(quad), m)).start()
            return c
        lax.fori_loop(1 if j == 0 else 0, 8, body, 0)

    def chunk_span(j):
        return pl.ds(((me_m - j + NMP) % NMP) * 8, 8)

    def quad_chunk(g, r_own, s_sib, r_sib, s_x, r_x, j):
        wait_bytes(g.at[0, pl.ds(0, 7 if j == 0 else 8)], recv.at[r_own + j])
        part = g.at[q, chunk_span(j)]
        rcopy(part, part, s_x, r_x + j, (xnb, me_m)).start()
        rcopy(part, part, s_sib, r_sib + j, (sib, me_m)).start()

    def quad_forward(g, r_x, s_f, r_f, j):
        part = g.at[q_x, chunk_span(j)]
        wait_bytes(part, recv.at[r_x + j])
        rcopy(part, part, s_f, r_f + j, (sib, me_m)).start()

    def project(g, flat, w, r_sib, r_f, j):
        m = (me_m - j + NMP) % NMP
        wait_bytes(g.at[0, pl.ds(0, 8)], recv.at[r_sib + j])
        wait_bytes(g.at[0, pl.ds(0, 8)], recv.at[r_f + j])
        for h in range(2):
            col = pl.multiple_of(m * 512 + h * 256, 256)
            part = g[:, pl.ds(m * 8, 8), h * 8:(h + 1) * 8, :].astype(F32).reshape(256, 256).astype(BF)
            flat[:, pl.ds(col, 256)] = part
            res = dot_nt(part, w[:, pl.ds(col, 256)])
            if j == 0 and h == 0:
                acc[...] = res
            else:
                acc[...] += res

    def part_chunk(rows, w, buf, landing, s, r, j):
        m = (me_m + j) % NMP
        for h in range(2):
            col = pl.multiple_of(m * 512 + h * 256, 256)
            res = dot(rows, w[:, pl.ds(col, 256)])
            buf[:, pl.ds(m * 8, 8), h * 8:(h + 1) * 8, :] = res.reshape(4, 8, 8, 256).astype(BF)
        span = pl.ds(m * 8, 8)
        rcopy(buf.at[q_d, span], landing.at[1, span], s, r + j, (sib, me_m)).start()
        rcopy(buf.at[q_sib, span], landing.at[0, span], s, r + j, (sib, me_m)).start()

    def pair_sum(buf, landing, out, far, r_sib, s, r, j):
        span = pl.ds(((me_m + j) % NMP) * 8, 8)
        wait_bytes(landing.at[pl.ds(0, 2), span], recv.at[r_sib + j])
        out[span] = (buf[q_x, span].astype(F32) + landing[1, span].astype(F32)).astype(BF)
        rcopy(out.at[span], far.at[span], s, r + j, (xnb, me_m)).start()

    def total_chunk(buf, landing, far, out, home, r_x, s, r, j):
        m = (me_m + j) % NMP
        span = pl.ds(m * 8, 8)
        wait_bytes(far.at[span], recv.at[r_x + j])
        out[span] = (buf[q, span].astype(F32) + landing[0, span].astype(F32)
                     + far[span].astype(F32)).astype(BF)

        def post(k, c):
            quad = (p4 + k) % 8
            rcopy(out.at[m * 8 + quad], home.at[u], s, r, (near_dp(quad), m)).start()
            return c
        lax.fori_loop(1 if j == 0 else 0, 8, post, 0)
        if j == 0:
            home[u] = out[u]

    mixing((x0, x1), mbuf, g_fwd)
    for j in range(CH):
        send_chunk(mbuf, g_fwd, S_M, R_M, j)
    wait_bytes(cin.at[pl.ds(0, 31)], recv.at[R_C])
    mixing((half(cin, 0, 256), half(cin, 1, 256)), bbuf, g_back)
    def weight_grad(out, lhs, rhs, m):
        out[:, m * 512:(m + 1) * 512] = dot(lhs[...], rhs[:, m * 512:(m + 1) * 512]).astype(BF)

    load_wi.wait()
    load_wo.wait()
    first = (pb, sb, xr, rb, pin, R_PX, S_PA, R_PA)
    second = (pb2, sb2, xr2, rb2, din, R_DX, S_DA, R_DA)
    quad_chunk(g_fwd, R_M, S_QSIB, R_QSIB, S_QX, R_QX, 0)
    send_chunk(bbuf, g_back, S_B, R_B, 0)
    quad_chunk(g_fwd, R_M, S_QSIB, R_QSIB, S_QX, R_QX, 1)
    send_chunk(bbuf, g_back, S_B, R_B, 1)
    quad_forward(g_fwd, R_QX, S_QF, R_QF, 0)
    quad_chunk(g_fwd, R_M, S_QSIB, R_QSIB, S_QX, R_QX, 2)
    send_chunk(bbuf, g_back, S_B, R_B, 2)
    quad_forward(g_fwd, R_QX, S_QF, R_QF, 1)
    project(g_fwd, xf, wi, R_QSIB, R_QF, 0)
    quad_chunk(g_fwd, R_M, S_QSIB, R_QSIB, S_QX, R_QX, 3)
    send_chunk(bbuf, g_back, S_B, R_B, 3)
    quad_forward(g_fwd, R_QX, S_QF, R_QF, 2)
    project(g_fwd, xf, wi, R_QSIB, R_QF, 1)
    quad_chunk(g_fwd, R_M, S_QSIB, R_QSIB, S_QX, R_QX, 4)
    send_chunk(bbuf, g_back, S_B, R_B, 4)
    quad_forward(g_fwd, R_QX, S_QF, R_QF, 3)
    project(g_fwd, xf, wi, R_QSIB, R_QF, 2)
    quad_chunk(g_fwd, R_M, S_QSIB, R_QSIB, S_QX, R_QX, 5)
    send_chunk(bbuf, g_back, S_B, R_B, 5)
    quad_forward(g_fwd, R_QX, S_QF, R_QF, 4)
    project(g_fwd, xf, wi, R_QSIB, R_QF, 3)
    quad_chunk(g_fwd, R_M, S_QSIB, R_QSIB, S_QX, R_QX, 6)
    send_chunk(bbuf, g_back, S_B, R_B, 6)
    quad_forward(g_fwd, R_QX, S_QF, R_QF, 5)
    project(g_fwd, xf, wi, R_QSIB, R_QF, 4)
    quad_chunk(g_fwd, R_M, S_QSIB, R_QSIB, S_QX, R_QX, 7)
    send_chunk(bbuf, g_back, S_B, R_B, 7)
    quad_forward(g_fwd, R_QX, S_QF, R_QF, 6)
    project(g_fwd, xf, wi, R_QSIB, R_QF, 5)
    quad_forward(g_fwd, R_QX, S_QF, R_QF, 7)
    quad_chunk(g_back, R_B, S_BSIB, R_BSIB, S_BX, R_BX, 0)
    project(g_fwd, xf, wi, R_QSIB, R_QF, 6)
    quad_chunk(g_back, R_B, S_BSIB, R_BSIB, S_BX, R_BX, 1)
    project(g_fwd, xf, wi, R_QSIB, R_QF, 7)
    quad_chunk(g_back, R_B, S_BSIB, R_BSIB, S_BX, R_BX, 2)
    pre = acc[...]
    sig = 1.0 / (1.0 + jnp.exp(-pre))
    act_f = pre * sig
    slope_s[...] = sig * (1.0 + pre * (1.0 - sig))
    rows_s[...] = act_f.astype(BF)
    lhs_s[...] = act_f.T.astype(BF)
    part_chunk(rows_s[...], wo, pb, sb, S_PSIB, R_PSIB, 0)
    part_chunk(rows_s[...], wo, pb, sb, S_PSIB, R_PSIB, 1)
    quad_chunk(g_back, R_B, S_BSIB, R_BSIB, S_BX, R_BX, 3)
    quad_forward(g_back, R_BX, S_BF, R_BF, 0)
    part_chunk(rows_s[...], wo, pb, sb, S_PSIB, R_PSIB, 2)
    part_chunk(rows_s[...], wo, pb, sb, S_PSIB, R_PSIB, 3)
    quad_chunk(g_back, R_B, S_BSIB, R_BSIB, S_BX, R_BX, 4)
    quad_forward(g_back, R_BX, S_BF, R_BF, 1)
    part_chunk(rows_s[...], wo, pb, sb, S_PSIB, R_PSIB, 4)
    part_chunk(rows_s[...], wo, pb, sb, S_PSIB, R_PSIB, 5)
    quad_chunk(g_back, R_B, S_BSIB, R_BSIB, S_BX, R_BX, 5)
    quad_forward(g_back, R_BX, S_BF, R_BF, 2)
    project(g_back, cf, wo, R_BSIB, R_BF, 0)
    part_chunk(rows_s[...], wo, pb, sb, S_PSIB, R_PSIB, 6)
    part_chunk(rows_s[...], wo, pb, sb, S_PSIB, R_PSIB, 7)
    quad_chunk(g_back, R_B, S_BSIB, R_BSIB, S_BX, R_BX, 6)
    quad_forward(g_back, R_BX, S_BF, R_BF, 3)
    project(g_back, cf, wo, R_BSIB, R_BF, 1)
    quad_chunk(g_back, R_B, S_BSIB, R_BSIB, S_BX, R_BX, 7)
    pair_sum(pb, sb, xsum, xr, R_PSIB, S_PX, R_PX, 0)
    pair_sum(pb, sb, xsum, xr, R_PSIB, S_PX, R_PX, 1)
    pair_sum(pb, sb, xsum, xr, R_PSIB, S_PX, R_PX, 2)
    pair_sum(pb, sb, xsum, xr, R_PSIB, S_PX, R_PX, 3)
    pair_sum(pb, sb, xsum, xr, R_PSIB, S_PX, R_PX, 4)
    pair_sum(pb, sb, xsum, xr, R_PSIB, S_PX, R_PX, 5)
    pair_sum(pb, sb, xsum, xr, R_PSIB, S_PX, R_PX, 6)
    pair_sum(pb, sb, xsum, xr, R_PSIB, S_PX, R_PX, 7)
    quad_forward(g_back, R_BX, S_BF, R_BF, 4)
    project(g_back, cf, wo, R_BSIB, R_BF, 2)
    quad_forward(g_back, R_BX, S_BF, R_BF, 5)
    project(g_back, cf, wo, R_BSIB, R_BF, 3)
    quad_forward(g_back, R_BX, S_BF, R_BF, 6)
    project(g_back, cf, wo, R_BSIB, R_BF, 4)
    quad_forward(g_back, R_BX, S_BF, R_BF, 7)
    project(g_back, cf, wo, R_BSIB, R_BF, 5)
    project(g_back, cf, wo, R_BSIB, R_BF, 6)
    project(g_back, cf, wo, R_BSIB, R_BF, 7)
    d_pre_f = acc[...] * slope_s[...]
    rows2_s[...] = d_pre_f.astype(BF)
    lhs2_s[...] = d_pre_f.T.astype(BF)
    total_chunk(*first, 0)
    part_chunk(rows2_s[...], wi, pb2, sb2, S_DSIB, R_DSIB, 0)
    weight_grad(o_wout, lhs_s, cf, 0)
    total_chunk(*first, 1)
    part_chunk(rows2_s[...], wi, pb2, sb2, S_DSIB, R_DSIB, 1)
    weight_grad(o_wout, lhs_s, cf, 1)
    total_chunk(*first, 2)
    part_chunk(rows2_s[...], wi, pb2, sb2, S_DSIB, R_DSIB, 2)
    pair_sum(pb2, sb2, xsum2, xr2, R_DSIB, S_DX, R_DX, 0)
    weight_grad(o_wout, lhs_s, cf, 2)
    total_chunk(*first, 3)
    part_chunk(rows2_s[...], wi, pb2, sb2, S_DSIB, R_DSIB, 3)
    pair_sum(pb2, sb2, xsum2, xr2, R_DSIB, S_DX, R_DX, 1)
    weight_grad(o_wout, lhs_s, cf, 3)
    total_chunk(*first, 4)
    part_chunk(rows2_s[...], wi, pb2, sb2, S_DSIB, R_DSIB, 4)
    pair_sum(pb2, sb2, xsum2, xr2, R_DSIB, S_DX, R_DX, 2)
    weight_grad(o_wout, lhs_s, cf, 4)
    total_chunk(*first, 5)
    part_chunk(rows2_s[...], wi, pb2, sb2, S_DSIB, R_DSIB, 5)
    pair_sum(pb2, sb2, xsum2, xr2, R_DSIB, S_DX, R_DX, 3)
    weight_grad(o_wout, lhs_s, cf, 5)
    total_chunk(*first, 6)
    part_chunk(rows2_s[...], wi, pb2, sb2, S_DSIB, R_DSIB, 6)
    pair_sum(pb2, sb2, xsum2, xr2, R_DSIB, S_DX, R_DX, 4)
    weight_grad(o_wout, lhs_s, cf, 6)
    total_chunk(*first, 7)
    part_chunk(rows2_s[...], wi, pb2, sb2, S_DSIB, R_DSIB, 7)
    pair_sum(pb2, sb2, xsum2, xr2, R_DSIB, S_DX, R_DX, 5)
    weight_grad(o_wout, lhs_s, cf, 7)
    pair_sum(pb2, sb2, xsum2, xr2, R_DSIB, S_DX, R_DX, 6)
    pair_sum(pb2, sb2, xsum2, xr2, R_DSIB, S_DX, R_DX, 7)
    total_chunk(*second, 0)
    weight_grad(o_win, lhs2_s, xf, 0)
    total_chunk(*second, 1)
    weight_grad(o_win, lhs2_s, xf, 1)
    total_chunk(*second, 2)
    weight_grad(o_win, lhs2_s, xf, 2)
    total_chunk(*second, 3)
    weight_grad(o_win, lhs2_s, xf, 3)
    total_chunk(*second, 4)
    weight_grad(o_win, lhs2_s, xf, 4)
    total_chunk(*second, 5)
    weight_grad(o_win, lhs2_s, xf, 5)
    total_chunk(*second, 6)
    weight_grad(o_win, lhs2_s, xf, 6)
    total_chunk(*second, 7)
    weight_grad(o_win, lhs2_s, xf, 7)

    wait_bytes(pin.at[pl.ds(0, 63)], recv.at[R_PA])
    for h in range(2):
        rows = half(pin, h, 512)
        res = dot_tn(amat[...], rows)
        osend[:, h * 8:(h + 1) * 8, :] = res.reshape(32, 8, 256).astype(BF)
        part = dot_nt(rows, half(cin, h, 256))
        if h == 0:
            bacc[...] = part
        else:
            bacc[...] += part
    oin[me_p] = osend[me_p]

    wait_bytes(din.at[pl.ds(0, 63)], recv.at[R_DA])
    back_rows = [half(din, h, 512) for h in range(2)]
    for h in range(2):
        bacc[...] += dot_nt(back_rows[h], half(xin, h, 256))
    wlsend[...] = jnp.sum(bacc[...].reshape(64, 8, 256) * m8[None], axis=1).reshape(8, 8, 256)
    send_col(wlsend, wlin, S_DW, R_DW, True)
    wlin[me_m] = wlsend[me_m]
    send_row(osend, oin, S_O, R_O, 1, 16)
    for h in range(2):
        bacc[h * 256:(h + 1) * 256, :] = dot_tn(amat[...], back_rows[h])
    wait_bytes(wlin.at[pl.ds(0, 7)], recv.at[R_DW])
    d_weight = jnp.sum(wlin[...], axis=0)
    prod = mix_own * d_weight
    mean = jnp.zeros((8, 256), F32)
    for g in range(8):
        mask = m8[g:g + 1, :]
        mean = mean + mask * jnp.sum(prod * mask, axis=1, keepdims=True)
    d_logit = mix_own * (d_weight - mean)
    dlsend[0:8, :] = d_logit[:, 0:128].astype(BF)
    dlsend[8:16, :] = d_logit[:, 128:256].astype(BF)
    send_col(dlsend, dlall, S_DL, R_DL, False)
    send_row(osend, oin, S_O, R_O, 16, NDP)
    dlall[me_m] = dlsend[...]
    wait_bytes(dlall.at[pl.ds(0, 7)], recv.at[R_DL])
    dl = jnp.concatenate([half(dlall, 0, 64), half(dlall, 1, 64)], axis=1)
    for h in range(2):
        part = dot(dl, half(xin, h, 256)).astype(BF)
        for e in range(4):
            for k in range(2):
                rsend[e * 4 + h * 2 + k] = part[e * 16:(e + 1) * 16, k * 128:(k + 1) * 128]
    reducer = me_p % 2 == 0
    mine = me_p // 2

    def send_tile(k, c):
        peer = (mine + k) % 16
        rcopy(rsend.at[peer], rin.at[me_p], S_R, R_R, (peer * 2, me_m)).start()
        return c
    lax.fori_loop(1, 16, send_tile, 0)

    @pl.when(me_p % 2 == 1)
    def _():
        rcopy(rsend.at[mine], rin.at[me_p], S_R, R_R, (mine * 2, me_m)).start()

    for h in range(2):
        res = bacc[h * 256:(h + 1) * 256, :] + dot_tn(dl, rt[:, h * 256:(h + 1) * 256])
        gsend[:, h * 8:(h + 1) * 8, :] = res.reshape(32, 8, 256).astype(BF)
    send_row(gsend, gin, S_G, R_G, 1, 16)
    gin[me_p] = gsend[me_p]

    def place(src, h):
        return dot_tn(perm, half(src, h, 256))

    wait_bytes(oin.at[pl.ds(0, 31)], recv.at[R_O])
    for h in range(2):
        o_mix[:, :, h * 256:(h + 1) * 256] = place(oin, h).reshape(4, 64, 256).astype(BF)

    @pl.when(reducer)
    def _():
        rin[me_p] = rsend[mine]
        wait_bytes(rin.at[pl.ds(0, 31)], recv.at[R_R])
        total = jnp.sum(rin[...].astype(F32), axis=0).astype(BF)
        rsum[...] = total
        rall[mine] = total

        def share(k, c):
            rcopy(rsum, rall.at[mine], S_RG, R_RG, ((me_p + k) % NDP, me_m)).start()
            return c
        lax.fori_loop(1, NDP, share, 0)

    send_row(gsend, gin, S_G, R_G, 16, NDP)
    wait_bytes(gin.at[pl.ds(0, 31)], recv.at[R_G])
    for h in range(2):
        cols = slice(h * 256, (h + 1) * 256)
        o_grad[:, :, cols] = place(gin, h).reshape(4, 64, 256).astype(BF)

    @pl.when(reducer)
    def _():
        wait_bytes(rall.at[pl.ds(0, 15)], recv.at[R_RG])

    @pl.when(me_p % 2 == 1)
    def _():
        wait_bytes(rall, recv.at[R_RG])

    for e in range(4):
        for k in range(4):
            o_router[e * 16:(e + 1) * 16, k * 128:(k + 1) * 128] = rall[e * 4 + k].astype(F32)

    @pl.when(me_p % 2 == 1)
    def _():
        wait_bytes(rsend, send.at[S_R])

    @pl.when(reducer)
    def _():
        wait_bytes(rsend.at[pl.ds(0, 15)], send.at[S_R])
        wait_bytes(rin.at[pl.ds(0, 31)], send.at[S_RG])

    for view, s in (
        (xs.at[pl.ds(0, 31)], S_X), (cs.at[pl.ds(0, 31)], S_C), (lin.at[pl.ds(0, 7)], S_L),
        (mixall.at[pl.ds(0, 7)], S_MIX), (mbuf.at[pl.ds(0, 63)], S_M), (bbuf.at[pl.ds(0, 63)], S_B),
        (g_fwd.at[0], S_QSIB), (g_fwd.at[0], S_QX), (g_fwd.at[0], S_QF),
        (g_back.at[0], S_BSIB), (g_back.at[0], S_BX), (g_back.at[0], S_BF),
        (sb, S_PSIB), (xsum, S_PX), (rb.at[pl.ds(0, 63)], S_PA),
        (sb2, S_DSIB), (xsum2, S_DX), (rb2.at[pl.ds(0, 63)], S_DA),
        (osend.at[pl.ds(0, 31)], S_O), (wlin.at[pl.ds(0, 7)], S_DW), (dlall.at[pl.ds(0, 7)], S_DL),
        (gsend.at[pl.ds(0, 31)], S_G),
    ):
        wait_bytes(view, send.at[s])


def copy_out(*refs):
    sems = refs[-1]
    moves = [pltpu.make_async_copy(refs[i], refs[5 + i], sems.at[i]) for i in (3, 4, 0, 1, 2)]
    for move in moves:
        move.start()
    for move in moves:
        move.wait()


def per_device(tokens, groups, router, w_in, w_out, cotangent):
    vm = lambda shape, dt=BF: pltpu.VMEM(shape, dt)
    blk32, blk64 = (32, 16, 256), (64, 16, 256)
    scratch = [
        vm((4, 64, 512)), vm((4, 64, 512)), vm((2, 128), jnp.int32), vm((64, 512)),
        vm(blk32), vm(blk32), vm(blk32), vm(blk32),
        vm((8, 8, 256), F32), vm((8, 8, 256), F32), vm((16, 128)), vm((8, 16, 128)), vm((512, 256)),
        vm(blk64), vm(blk64),
        vm((4,) + blk64), vm((4,) + blk64), vm((256, 4096)), vm((256, 4096)),
        vm((256, 4096)), vm((256, 4096)),
        vm((4,) + blk64), vm((2,) + blk64), vm(blk64), vm(blk64), vm(blk64), vm(blk64),
        vm((4,) + blk64), vm((2,) + blk64), vm(blk64), vm(blk64), vm(blk64), vm(blk64),
        vm(blk32), vm(blk32), vm(blk32), vm(blk32),
        vm((8, 8, 256), F32), vm((8, 8, 256), F32), vm((16, 128)), vm((8, 16, 128)), vm((512, 256), F32), vm((256, 256), F32),
        vm((256, 256)), vm((256, 256)), vm((256, 256)), vm((256, 256)),
        vm((16, 16, 128)), vm((32, 16, 128)), vm((16, 16, 128)), vm((16, 128)),
        vm((256, 256), F32),
        pltpu.SemaphoreType.DMA((N_SEND,)), pltpu.SemaphoreType.DMA((N_RECV,)),
        pltpu.SemaphoreType.DMA((6,)),
    ]
    in_vmem = pl.BlockSpec(memory_space=pltpu.VMEM)
    anywhere = pl.BlockSpec(memory_space=pl.ANY)
    in_hbm = pl.BlockSpec(memory_space=pltpu.HBM)
    shapes = (
        jax.ShapeDtypeStruct((4, 64, 512), BF),
        jax.ShapeDtypeStruct((4, 64, 512), BF),
        jax.ShapeDtypeStruct((64, 512), F32),
        jax.ShapeDtypeStruct((256, 4096), BF),
        jax.ShapeDtypeStruct((256, 4096), BF),
    )
    results = pl.pallas_call(
        kernel,
        out_shape=shapes,
        in_specs=[in_hbm] * 6,
        out_specs=[in_vmem] * 5,
        scratch_shapes=scratch,
        compiler_params=pltpu.CompilerParams(
            collective_id=0, has_side_effects=True, vmem_limit_bytes=44 * 1024 * 1024),
        cost_estimate=pl.CostEstimate(flops=4 * 10**9, bytes_accessed=10**7, transcendentals=10**5),
    )(*[pltpu.with_memory_space_constraint(a, pltpu.HBM)
        for a in (tokens, cotangent, groups, router.T, w_in, w_out)])
    mixed_out, tokens_grad, router_t, g_in, g_out = pl.pallas_call(
        copy_out,
        out_shape=shapes,
        in_specs=[anywhere] * 5,
        out_specs=[anywhere] * 5,
        scratch_shapes=[pltpu.SemaphoreType.DMA((5,))],
        compiler_params=pltpu.CompilerParams(vmem_limit_bytes=2 * 1024 * 1024),
    )(*results)
    return mixed_out, tokens_grad, router_t.T, g_in, g_out


def solution(mesh):
    return jax.shard_map(
        per_device,
        mesh=mesh,
        in_specs=(
            P("dp", None, "mp"),
            P("dp", None),
            P("mp", None),
            P(("mp", "dp"), None),
            P(("mp", "dp"), None),
            P("dp", None, "mp"),
        ),
        out_specs=(
            P("dp", None, "mp"),
            P("dp", None, "mp"),
            P("mp", None),
            P(("mp", "dp"), None),
            P(("mp", "dp"), None),
        ),
        check_vma=False,
    )
```

```python
import jax
import jax.numpy as jnp
from jax import lax
from jax.experimental import pallas as pl
from jax.experimental.pallas import tpu as pltpu
from jax.sharding import PartitionSpec as P

MESH = pl.DeviceIdType.MESH
BF = jnp.bfloat16
F32 = jnp.float32
NDP = 32
NMP = 8
CH = 8

NT = (((1,), (1,)), ((), ()))
TN = (((0,), (0,)), ((), ()))


def dot(a, b):
    return jnp.dot(a, b, preferred_element_type=F32)


def dot_nt(a, b):
    return lax.dot_general(a, b, NT, preferred_element_type=F32)


def dot_tn(a, b):
    return lax.dot_general(a, b, TN, preferred_element_type=F32)


def iota(shape, dim):
    return lax.broadcasted_iota(jnp.int32, shape, dim)


def wait_bytes(view, sem):
    pltpu.make_async_copy(view, view, sem).wait()


(S_X, S_C, S_L, S_MIX, S_M, S_B, S_QSIB, S_QX, S_QF, S_BSIB, S_BX, S_BF) = range(12)
S_PSIB, S_PX, S_PA, S_DSIB, S_DX, S_DA, S_O, S_DW, S_DL, S_G, S_R, S_RG = range(12, 24)
N_SEND = 24
R_X, R_C, R_L, R_MIX, R_PA, R_DA, R_O, R_DW, R_DL, R_G, R_R, R_RG = range(12)
(R_M, R_B, R_QSIB, R_QX, R_QF, R_BSIB, R_BX, R_BF, R_PSIB, R_PX, R_DSIB, R_DX) = range(12, 108, 8)
N_RECV = 108


def kernel(tok_in, cot_in, grp_in, rt_in, w_in, w_out,
           o_mix, o_grad, o_router, o_win, o_wout,
           tok, cot, grp, rt, xs, cs, xin, cin, lsend, lin, mixsend, mixall, amat, mbuf, bbuf,
           g_fwd, g_back, xf, cf, wi, wo, pb, sb, xsum, xr, rb, pin,
           pb2, sb2, xsum2, xr2, rb2, din, osend, oin, gsend, gin,
           wlsend, wlin, dlsend, dlall, bacc, slope_s, rows_s, rows2_s, lhs_s, lhs2_s, rsend, rin, rall, rsum, acc,
           send, recv, wsem):
    me_p = lax.axis_index("dp")
    me_m = lax.axis_index("mp")
    p4 = me_p // 4
    q = me_p % 4
    u = me_m * 8 + p4
    sib = me_p + 1 - 2 * (me_p % 2)
    xnb = me_p + 2 - 4 * (q // 2)
    q_sib = q + 1 - 2 * (q % 2)
    q_x = q + 2 - 4 * (q // 2)
    q_d = q_sib + 2 - 4 * (q_sib // 2)

    def near_q(quad):
        return ((q // 2 + quad + p4) % 2) * 2 + q % 2

    def near_dp(quad):
        return quad * 4 + near_q(quad)

    def rcopy(src, dst, s, r, dev):
        return pltpu.make_async_remote_copy(
            src_ref=src, dst_ref=dst, send_sem=send.at[s], recv_sem=recv.at[r],
            device_id=dev, device_id_type=MESH)

    load_wi = pltpu.make_async_copy(w_in, wi, wsem.at[0])
    load_wo = pltpu.make_async_copy(w_out, wo, wsem.at[1])
    load_tok = pltpu.make_async_copy(tok_in, tok, wsem.at[2])
    load_cot = pltpu.make_async_copy(cot_in, cot, wsem.at[3])
    load_grp = pltpu.make_async_copy(grp_in, grp, wsem.at[4])
    load_rt = pltpu.make_async_copy(rt_in, rt, wsem.at[5])
    load_tok.start()
    load_grp.start()
    load_rt.start()
    load_cot.start()

    bar = pltpu.get_barrier_semaphore()

    def sig_row(k, c):
        pl.semaphore_signal(bar, inc=1, device_id=((me_p + k) % NDP, me_m), device_id_type=MESH)
        return c

    lax.fori_loop(1, NDP, sig_row, 0)

    def sig_col(k, c):
        pl.semaphore_signal(bar, inc=1, device_id=(me_p, (me_m + k) % NMP), device_id_type=MESH)
        return c

    lax.fori_loop(1, NMP, sig_col, 0)

    r_i = iota((256, 256), 0)
    c_i = iota((256, 256), 1)
    src_row = ((r_i // 2) % 4) * 64 + (r_i // 8) * 2 + r_i % 2
    perm = (c_i == src_row).astype(F32).astype(BF)

    def blocks(ref, out):
        rows = ref[...].reshape(256, 512)
        for h in range(2):
            res = dot(perm, rows[:, h * 256:(h + 1) * 256])
            out[:, h * 8:(h + 1) * 8, :] = res.reshape(32, 8, 256).astype(BF)

    def send_row(src, dst, s, r, low=1, high=NDP):
        def body(k, c):
            peer = (me_p + k) % NDP
            rcopy(src.at[peer], dst.at[me_p], s, r, (peer, me_m)).start()
            return c
        lax.fori_loop(low, high, body, 0)

    def send_col(src, dst, s, r, spread):
        def body(k, c):
            peer = (me_m + k) % NMP
            part = src.at[peer] if spread else src
            rcopy(part, dst.at[me_m], s, r, (me_p, peer)).start()
            return c
        lax.fori_loop(1, NMP, body, 0)

    load_tok.wait()
    blocks(tok, xs)
    pl.semaphore_wait(bar, 31 + 7)
    send_row(xs, xin, S_X, R_X)
    load_cot.wait()
    blocks(cot, cs)
    send_row(cs, cin, S_C, R_C)
    load_wi.start()
    load_wo.start()
    load_grp.wait()
    load_rt.wait()
    xin[me_p] = xs[me_p]
    cin[me_p] = cs[me_p]

    t_i = iota((256, 128), 0)
    l_i = iota((256, 128), 1)
    order = jnp.where(t_i % 2 == 0, grp[0:1, :], grp[1:2, :])
    hit = (order == t_i // 2).astype(F32).astype(BF)
    g_i = iota((8, 128), 0)
    s_i = iota((8, 128), 1)
    pick = (s_i // 32 == g_i % 4).astype(F32).astype(BF)
    own_pos = (iota((8, 256), 1) % 2 == iota((8, 256), 0) // 4).astype(F32)
    m8 = dot_nt(pick, hit) * own_pos

    def half(ref, h, rows):
        return ref[:, h * 8:(h + 1) * 8, :].astype(F32).reshape(rows, ref.shape[-1]).astype(BF)

    wait_bytes(xin.at[pl.ds(0, 31)], recv.at[R_X])
    x0, x1 = half(xin, 0, 256), half(xin, 1, 256)
    r0, r1 = rt[:, 0:256], rt[:, 256:512]
    lsend[...] = (dot_nt(r0, x0) + dot_nt(r1, x1)).reshape(8, 8, 256)
    send_col(lsend, lin, S_L, R_L, True)
    lin[me_m] = lsend[me_m]
    wait_bytes(lin.at[pl.ds(0, 7)], recv.at[R_L])
    logit = jnp.sum(lin[...], axis=0)
    big = jnp.full((8, 256), -jnp.inf, F32)
    peak = jnp.zeros((8, 256), F32)
    for g in range(8):
        inside = jnp.broadcast_to(m8[g:g + 1, :] > 0.5, (8, 256))
        top = jnp.max(jnp.where(inside, logit, big), axis=1, keepdims=True)
        peak = jnp.where(inside, top, peak)
    ex = jnp.exp(logit - peak)
    den = jnp.zeros((8, 256), F32)
    for g in range(8):
        mask = m8[g:g + 1, :]
        den = den + mask * jnp.sum(ex * mask, axis=1, keepdims=True)
    mix_own = ex / den
    mixsend[0:8, :] = mix_own[:, 0:128].astype(BF)
    mixsend[8:16, :] = mix_own[:, 128:256].astype(BF)
    send_col(mixsend, mixall, S_MIX, R_MIX, False)
    mixall[me_m] = mixsend[...]
    wait_bytes(mixall.at[pl.ds(0, 7)], recv.at[R_MIX])

    spread = (iota((512, 64), 0) // 8 == iota((512, 64), 1)).astype(F32).astype(BF)
    for h in range(2):
        wide = dot(spread, half(mixall, h, 64)).reshape(64, 8, 128)
        sel = wide * m8[:, h * 128:(h + 1) * 128][None]
        amat[:, h * 128:(h + 1) * 128] = sel.reshape(512, 128).astype(BF)

    def mixing(rows, buf, dst):
        for h in range(2):
            res = dot(amat[...], rows[h])
            buf[:, h * 8:(h + 1) * 8, :] = res.reshape(64, 8, 256).astype(BF)
        dst[q, u] = buf[u]

    def send_chunk(src, dst, s, r, j):
        m = (me_m + j) % NMP

        def body(k, c):
            quad = (p4 + k) % 8
            rcopy(src.at[m * 8 + quad], dst.at[near_q(quad), u], s, r + j, (near_dp(quad), m)).start()
            return c
        lax.fori_loop(1 if j == 0 else 0, 8, body, 0)

    def chunk_span(j):
        return pl.ds(((me_m - j + NMP) % NMP) * 8, 8)

    def quad_chunk(g, r_own, s_sib, r_sib, s_x, r_x, j):
        wait_bytes(g.at[0, pl.ds(0, 7 if j == 0 else 8)], recv.at[r_own + j])
        part = g.at[q, chunk_span(j)]
        rcopy(part, part, s_x, r_x + j, (xnb, me_m)).start()
        rcopy(part, part, s_sib, r_sib + j, (sib, me_m)).start()

    def quad_forward(g, r_x, s_f, r_f, j):
        part = g.at[q_x, chunk_span(j)]
        wait_bytes(part, recv.at[r_x + j])
        rcopy(part, part, s_f, r_f + j, (sib, me_m)).start()

    def project(g, flat, w, r_sib, r_f, j):
        m = (me_m - j + NMP) % NMP
        wait_bytes(g.at[0, pl.ds(0, 8)], recv.at[r_sib + j])
        wait_bytes(g.at[0, pl.ds(0, 8)], recv.at[r_f + j])
        for h in range(2):
            col = pl.multiple_of(m * 512 + h * 256, 256)
            part = g[:, pl.ds(m * 8, 8), h * 8:(h + 1) * 8, :].astype(F32).reshape(256, 256).astype(BF)
            flat[:, pl.ds(col, 256)] = part
            res = dot_nt(part, w[:, pl.ds(col, 256)])
            if j == 0 and h == 0:
                acc[...] = res
            else:
                acc[...] += res

    def part_chunk(rows, w, buf, landing, s, r, j):
        m = (me_m + j) % NMP
        for h in range(2):
            col = pl.multiple_of(m * 512 + h * 256, 256)
            res = dot(rows, w[:, pl.ds(col, 256)])
            buf[:, pl.ds(m * 8, 8), h * 8:(h + 1) * 8, :] = res.reshape(4, 8, 8, 256).astype(BF)
        span = pl.ds(m * 8, 8)
        rcopy(buf.at[q_d, span], landing.at[1, span], s, r + j, (sib, me_m)).start()
        rcopy(buf.at[q_sib, span], landing.at[0, span], s, r + j, (sib, me_m)).start()

    def pair_sum(buf, landing, out, far, r_sib, s, r, j):
        span = pl.ds(((me_m + j) % NMP) * 8, 8)
        wait_bytes(landing.at[pl.ds(0, 2), span], recv.at[r_sib + j])
        out[span] = (buf[q_x, span].astype(F32) + landing[1, span].astype(F32)).astype(BF)
        rcopy(out.at[span], far.at[span], s, r + j, (xnb, me_m)).start()

    def total_chunk(buf, landing, far, out, home, r_x, s, r, j):
        m = (me_m + j) % NMP
        span = pl.ds(m * 8, 8)
        wait_bytes(far.at[span], recv.at[r_x + j])
        out[span] = (buf[q, span].astype(F32) + landing[0, span].astype(F32)
                     + far[span].astype(F32)).astype(BF)

        def post(k, c):
            quad = (p4 + k) % 8
            rcopy(out.at[m * 8 + quad], home.at[u], s, r, (near_dp(quad), m)).start()
            return c
        lax.fori_loop(1 if j == 0 else 0, 8, post, 0)
        if j == 0:
            home[u] = out[u]

    mixing((x0, x1), mbuf, g_fwd)
    for j in range(CH):
        send_chunk(mbuf, g_fwd, S_M, R_M, j)
    wait_bytes(cin.at[pl.ds(0, 31)], recv.at[R_C])
    mixing((half(cin, 0, 256), half(cin, 1, 256)), bbuf, g_back)
    def weight_grad(out, lhs, rhs, m):
        out[:, m * 512:(m + 1) * 512] = dot(lhs[...], rhs[:, m * 512:(m + 1) * 512]).astype(BF)

    load_wi.wait()
    load_wo.wait()
    first = (pb, sb, xr, rb, pin, R_PX, S_PA, R_PA)
    second = (pb2, sb2, xr2, rb2, din, R_DX, S_DA, R_DA)
    quad_chunk(g_fwd, R_M, S_QSIB, R_QSIB, S_QX, R_QX, 0)
    send_chunk(bbuf, g_back, S_B, R_B, 0)
    quad_chunk(g_fwd, R_M, S_QSIB, R_QSIB, S_QX, R_QX, 1)
    send_chunk(bbuf, g_back, S_B, R_B, 1)
    quad_forward(g_fwd, R_QX, S_QF, R_QF, 0)
    quad_chunk(g_fwd, R_M, S_QSIB, R_QSIB, S_QX, R_QX, 2)
    send_chunk(bbuf, g_back, S_B, R_B, 2)
    quad_forward(g_fwd, R_QX, S_QF, R_QF, 1)
    project(g_fwd, xf, wi, R_QSIB, R_QF, 0)
    quad_chunk(g_fwd, R_M, S_QSIB, R_QSIB, S_QX, R_QX, 3)
    send_chunk(bbuf, g_back, S_B, R_B, 3)
    quad_forward(g_fwd, R_QX, S_QF, R_QF, 2)
    project(g_fwd, xf, wi, R_QSIB, R_QF, 1)
    quad_chunk(g_fwd, R_M, S_QSIB, R_QSIB, S_QX, R_QX, 4)
    send_chunk(bbuf, g_back, S_B, R_B, 4)
    quad_forward(g_fwd, R_QX, S_QF, R_QF, 3)
    project(g_fwd, xf, wi, R_QSIB, R_QF, 2)
    quad_chunk(g_fwd, R_M, S_QSIB, R_QSIB, S_QX, R_QX, 5)
    send_chunk(bbuf, g_back, S_B, R_B, 5)
    quad_forward(g_fwd, R_QX, S_QF, R_QF, 4)
    project(g_fwd, xf, wi, R_QSIB, R_QF, 3)
    quad_chunk(g_fwd, R_M, S_QSIB, R_QSIB, S_QX, R_QX, 6)
    send_chunk(bbuf, g_back, S_B, R_B, 6)
    quad_forward(g_fwd, R_QX, S_QF, R_QF, 5)
    project(g_fwd, xf, wi, R_QSIB, R_QF, 4)
    quad_chunk(g_fwd, R_M, S_QSIB, R_QSIB, S_QX, R_QX, 7)
    send_chunk(bbuf, g_back, S_B, R_B, 7)
    quad_forward(g_fwd, R_QX, S_QF, R_QF, 6)
    project(g_fwd, xf, wi, R_QSIB, R_QF, 5)
    quad_forward(g_fwd, R_QX, S_QF, R_QF, 7)
    quad_chunk(g_back, R_B, S_BSIB, R_BSIB, S_BX, R_BX, 0)
    project(g_fwd, xf, wi, R_QSIB, R_QF, 6)
    quad_chunk(g_back, R_B, S_BSIB, R_BSIB, S_BX, R_BX, 1)
    project(g_fwd, xf, wi, R_QSIB, R_QF, 7)
    quad_chunk(g_back, R_B, S_BSIB, R_BSIB, S_BX, R_BX, 2)
    pre = acc[...]
    sig = 1.0 / (1.0 + jnp.exp(-pre))
    act_f = pre * sig
    slope_s[...] = sig * (1.0 + pre * (1.0 - sig))
    rows_s[...] = act_f.astype(BF)
    lhs_s[...] = act_f.T.astype(BF)
    part_chunk(rows_s[...], wo, pb, sb, S_PSIB, R_PSIB, 0)
    part_chunk(rows_s[...], wo, pb, sb, S_PSIB, R_PSIB, 1)
    quad_chunk(g_back, R_B, S_BSIB, R_BSIB, S_BX, R_BX, 3)
    quad_forward(g_back, R_BX, S_BF, R_BF, 0)
    part_chunk(rows_s[...], wo, pb, sb, S_PSIB, R_PSIB, 2)
    part_chunk(rows_s[...], wo, pb, sb, S_PSIB, R_PSIB, 3)
    quad_chunk(g_back, R_B, S_BSIB, R_BSIB, S_BX, R_BX, 4)
    quad_forward(g_back, R_BX, S_BF, R_BF, 1)
    part_chunk(rows_s[...], wo, pb, sb, S_PSIB, R_PSIB, 4)
    part_chunk(rows_s[...], wo, pb, sb, S_PSIB, R_PSIB, 5)
    quad_chunk(g_back, R_B, S_BSIB, R_BSIB, S_BX, R_BX, 5)
    quad_forward(g_back, R_BX, S_BF, R_BF, 2)
    project(g_back, cf, wo, R_BSIB, R_BF, 0)
    part_chunk(rows_s[...], wo, pb, sb, S_PSIB, R_PSIB, 6)
    part_chunk(rows_s[...], wo, pb, sb, S_PSIB, R_PSIB, 7)
    quad_chunk(g_back, R_B, S_BSIB, R_BSIB, S_BX, R_BX, 6)
    quad_forward(g_back, R_BX, S_BF, R_BF, 3)
    project(g_back, cf, wo, R_BSIB, R_BF, 1)
    quad_chunk(g_back, R_B, S_BSIB, R_BSIB, S_BX, R_BX, 7)
    pair_sum(pb, sb, xsum, xr, R_PSIB, S_PX, R_PX, 0)
    pair_sum(pb, sb, xsum, xr, R_PSIB, S_PX, R_PX, 1)
    pair_sum(pb, sb, xsum, xr, R_PSIB, S_PX, R_PX, 2)
    pair_sum(pb, sb, xsum, xr, R_PSIB, S_PX, R_PX, 3)
    pair_sum(pb, sb, xsum, xr, R_PSIB, S_PX, R_PX, 4)
    pair_sum(pb, sb, xsum, xr, R_PSIB, S_PX, R_PX, 5)
    pair_sum(pb, sb, xsum, xr, R_PSIB, S_PX, R_PX, 6)
    pair_sum(pb, sb, xsum, xr, R_PSIB, S_PX, R_PX, 7)
    quad_forward(g_back, R_BX, S_BF, R_BF, 4)
    project(g_back, cf, wo, R_BSIB, R_BF, 2)
    quad_forward(g_back, R_BX, S_BF, R_BF, 5)
    project(g_back, cf, wo, R_BSIB, R_BF, 3)
    quad_forward(g_back, R_BX, S_BF, R_BF, 6)
    project(g_back, cf, wo, R_BSIB, R_BF, 4)
    quad_forward(g_back, R_BX, S_BF, R_BF, 7)
    project(g_back, cf, wo, R_BSIB, R_BF, 5)
    project(g_back, cf, wo, R_BSIB, R_BF, 6)
    project(g_back, cf, wo, R_BSIB, R_BF, 7)
    d_pre_f = acc[...] * slope_s[...]
    rows2_s[...] = d_pre_f.astype(BF)
    lhs2_s[...] = d_pre_f.T.astype(BF)
    total_chunk(*first, 0)
    part_chunk(rows2_s[...], wi, pb2, sb2, S_DSIB, R_DSIB, 0)
    weight_grad(o_wout, lhs_s, cf, 0)
    total_chunk(*first, 1)
    part_chunk(rows2_s[...], wi, pb2, sb2, S_DSIB, R_DSIB, 1)
    weight_grad(o_wout, lhs_s, cf, 1)
    total_chunk(*first, 2)
    part_chunk(rows2_s[...], wi, pb2, sb2, S_DSIB, R_DSIB, 2)
    pair_sum(pb2, sb2, xsum2, xr2, R_DSIB, S_DX, R_DX, 0)
    weight_grad(o_wout, lhs_s, cf, 2)
    total_chunk(*first, 3)
    part_chunk(rows2_s[...], wi, pb2, sb2, S_DSIB, R_DSIB, 3)
    pair_sum(pb2, sb2, xsum2, xr2, R_DSIB, S_DX, R_DX, 1)
    weight_grad(o_wout, lhs_s, cf, 3)
    total_chunk(*first, 4)
    part_chunk(rows2_s[...], wi, pb2, sb2, S_DSIB, R_DSIB, 4)
    pair_sum(pb2, sb2, xsum2, xr2, R_DSIB, S_DX, R_DX, 2)
    weight_grad(o_wout, lhs_s, cf, 4)
    total_chunk(*first, 5)
    part_chunk(rows2_s[...], wi, pb2, sb2, S_DSIB, R_DSIB, 5)
    pair_sum(pb2, sb2, xsum2, xr2, R_DSIB, S_DX, R_DX, 3)
    weight_grad(o_wout, lhs_s, cf, 5)
    total_chunk(*first, 6)
    part_chunk(rows2_s[...], wi, pb2, sb2, S_DSIB, R_DSIB, 6)
    pair_sum(pb2, sb2, xsum2, xr2, R_DSIB, S_DX, R_DX, 4)
    weight_grad(o_wout, lhs_s, cf, 6)
    total_chunk(*first, 7)
    part_chunk(rows2_s[...], wi, pb2, sb2, S_DSIB, R_DSIB, 7)
    pair_sum(pb2, sb2, xsum2, xr2, R_DSIB, S_DX, R_DX, 5)
    weight_grad(o_wout, lhs_s, cf, 7)
    pair_sum(pb2, sb2, xsum2, xr2, R_DSIB, S_DX, R_DX, 6)
    pair_sum(pb2, sb2, xsum2, xr2, R_DSIB, S_DX, R_DX, 7)
    total_chunk(*second, 0)
    weight_grad(o_win, lhs2_s, xf, 0)
    total_chunk(*second, 1)
    weight_grad(o_win, lhs2_s, xf, 1)
    total_chunk(*second, 2)
    weight_grad(o_win, lhs2_s, xf, 2)
    total_chunk(*second, 3)
    weight_grad(o_win, lhs2_s, xf, 3)
    total_chunk(*second, 4)
    weight_grad(o_win, lhs2_s, xf, 4)
    total_chunk(*second, 5)
    weight_grad(o_win, lhs2_s, xf, 5)
    total_chunk(*second, 6)
    weight_grad(o_win, lhs2_s, xf, 6)
    total_chunk(*second, 7)
    weight_grad(o_win, lhs2_s, xf, 7)

    wait_bytes(pin.at[pl.ds(0, 63)], recv.at[R_PA])
    for h in range(2):
        rows = half(pin, h, 512)
        res = dot_tn(amat[...], rows)
        osend[:, h * 8:(h + 1) * 8, :] = res.reshape(32, 8, 256).astype(BF)
        part = dot_nt(rows, half(cin, h, 256))
        if h == 0:
            bacc[...] = part
        else:
            bacc[...] += part
    oin[me_p] = osend[me_p]

    wait_bytes(din.at[pl.ds(0, 63)], recv.at[R_DA])
    back_rows = [half(din, h, 512) for h in range(2)]
    for h in range(2):
        bacc[...] += dot_nt(back_rows[h], half(xin, h, 256))
    wlsend[...] = jnp.sum(bacc[...].reshape(64, 8, 256) * m8[None], axis=1).reshape(8, 8, 256)
    send_col(wlsend, wlin, S_DW, R_DW, True)
    wlin[me_m] = wlsend[me_m]
    send_row(osend, oin, S_O, R_O, 1, 16)
    for h in range(2):
        bacc[h * 256:(h + 1) * 256, :] = dot_tn(amat[...], back_rows[h])
    wait_bytes(wlin.at[pl.ds(0, 7)], recv.at[R_DW])
    d_weight = jnp.sum(wlin[...], axis=0)
    prod = mix_own * d_weight
    mean = jnp.zeros((8, 256), F32)
    for g in range(8):
        mask = m8[g:g + 1, :]
        mean = mean + mask * jnp.sum(prod * mask, axis=1, keepdims=True)
    d_logit = mix_own * (d_weight - mean)
    dlsend[0:8, :] = d_logit[:, 0:128].astype(BF)
    dlsend[8:16, :] = d_logit[:, 128:256].astype(BF)
    send_col(dlsend, dlall, S_DL, R_DL, False)
    send_row(osend, oin, S_O, R_O, 16, NDP)
    dlall[me_m] = dlsend[...]
    wait_bytes(dlall.at[pl.ds(0, 7)], recv.at[R_DL])
    dl = jnp.concatenate([half(dlall, 0, 64), half(dlall, 1, 64)], axis=1)
    for h in range(2):
        part = dot(dl, half(xin, h, 256)).astype(BF)
        for e in range(4):
            for k in range(2):
                rsend[e * 4 + h * 2 + k] = part[e * 16:(e + 1) * 16, k * 128:(k + 1) * 128]
    reducer = me_p % 2 == 0
    mine = me_p // 2

    def send_tile(k, c):
        peer = (mine + k) % 16
        rcopy(rsend.at[peer], rin.at[me_p], S_R, R_R, (peer * 2, me_m)).start()
        return c
    lax.fori_loop(1, 16, send_tile, 0)

    @pl.when(me_p % 2 == 1)
    def _():
        rcopy(rsend.at[mine], rin.at[me_p], S_R, R_R, (mine * 2, me_m)).start()

    for h in range(2):
        res = bacc[h * 256:(h + 1) * 256, :] + dot_tn(dl, rt[:, h * 256:(h + 1) * 256])
        gsend[:, h * 8:(h + 1) * 8, :] = res.reshape(32, 8, 256).astype(BF)
    send_row(gsend, gin, S_G, R_G, 1, 16)
    gin[me_p] = gsend[me_p]

    def place(src, h):
        return dot_tn(perm, half(src, h, 256))

    @pl.when(reducer)
    def _():
        rin[me_p] = rsend[mine]
        wait_bytes(rin.at[pl.ds(0, 31)], recv.at[R_R])
        total = jnp.sum(rin[...].astype(F32), axis=0).astype(BF)
        rsum[...] = total
        rall[mine] = total

        def share(k, c):
            rcopy(rsum, rall.at[mine], S_RG, R_RG, ((me_p + k) % NDP, me_m)).start()
            return c
        lax.fori_loop(1, NDP, share, 0)

    send_row(gsend, gin, S_G, R_G, 16, NDP)

    wait_bytes(oin.at[pl.ds(0, 31)], recv.at[R_O])
    for h in range(2):
        o_mix[:, :, h * 256:(h + 1) * 256] = place(oin, h).reshape(4, 64, 256).astype(BF)

    wait_bytes(gin.at[pl.ds(0, 31)], recv.at[R_G])
    for h in range(2):
        cols = slice(h * 256, (h + 1) * 256)
        o_grad[:, :, cols] = place(gin, h).reshape(4, 64, 256).astype(BF)

    @pl.when(reducer)
    def _():
        wait_bytes(rall.at[pl.ds(0, 15)], recv.at[R_RG])

    @pl.when(me_p % 2 == 1)
    def _():
        wait_bytes(rall, recv.at[R_RG])

    for e in range(4):
        for k in range(4):
            o_router[e * 16:(e + 1) * 16, k * 128:(k + 1) * 128] = rall[e * 4 + k].astype(F32)

    @pl.when(me_p % 2 == 1)
    def _():
        wait_bytes(rsend, send.at[S_R])

    @pl.when(reducer)
    def _():
        wait_bytes(rsend.at[pl.ds(0, 15)], send.at[S_R])
        wait_bytes(rin.at[pl.ds(0, 31)], send.at[S_RG])

    for view, s in (
        (xs.at[pl.ds(0, 31)], S_X), (cs.at[pl.ds(0, 31)], S_C), (lin.at[pl.ds(0, 7)], S_L),
        (mixall.at[pl.ds(0, 7)], S_MIX), (mbuf.at[pl.ds(0, 63)], S_M), (bbuf.at[pl.ds(0, 63)], S_B),
        (g_fwd.at[0], S_QSIB), (g_fwd.at[0], S_QX), (g_fwd.at[0], S_QF),
        (g_back.at[0], S_BSIB), (g_back.at[0], S_BX), (g_back.at[0], S_BF),
        (sb, S_PSIB), (xsum, S_PX), (rb.at[pl.ds(0, 63)], S_PA),
        (sb2, S_DSIB), (xsum2, S_DX), (rb2.at[pl.ds(0, 63)], S_DA),
        (osend.at[pl.ds(0, 31)], S_O), (wlin.at[pl.ds(0, 7)], S_DW), (dlall.at[pl.ds(0, 7)], S_DL),
        (gsend.at[pl.ds(0, 31)], S_G),
    ):
        wait_bytes(view, send.at[s])


def copy_out(*refs):
    sems = refs[-1]
    moves = [pltpu.make_async_copy(refs[i], refs[5 + i], sems.at[i]) for i in (3, 4, 0, 1, 2)]
    for move in moves:
        move.start()
    for move in moves:
        move.wait()


def per_device(tokens, groups, router, w_in, w_out, cotangent):
    vm = lambda shape, dt=BF: pltpu.VMEM(shape, dt)
    blk32, blk64 = (32, 16, 256), (64, 16, 256)
    scratch = [
        vm((4, 64, 512)), vm((4, 64, 512)), vm((2, 128), jnp.int32), vm((64, 512)),
        vm(blk32), vm(blk32), vm(blk32), vm(blk32),
        vm((8, 8, 256), F32), vm((8, 8, 256), F32), vm((16, 128)), vm((8, 16, 128)), vm((512, 256)),
        vm(blk64), vm(blk64),
        vm((4,) + blk64), vm((4,) + blk64), vm((256, 4096)), vm((256, 4096)),
        vm((256, 4096)), vm((256, 4096)),
        vm((4,) + blk64), vm((2,) + blk64), vm(blk64), vm(blk64), vm(blk64), vm(blk64),
        vm((4,) + blk64), vm((2,) + blk64), vm(blk64), vm(blk64), vm(blk64), vm(blk64),
        vm(blk32), vm(blk32), vm(blk32), vm(blk32),
        vm((8, 8, 256), F32), vm((8, 8, 256), F32), vm((16, 128)), vm((8, 16, 128)), vm((512, 256), F32), vm((256, 256), F32),
        vm((256, 256)), vm((256, 256)), vm((256, 256)), vm((256, 256)),
        vm((16, 16, 128)), vm((32, 16, 128)), vm((16, 16, 128)), vm((16, 128)),
        vm((256, 256), F32),
        pltpu.SemaphoreType.DMA((N_SEND,)), pltpu.SemaphoreType.DMA((N_RECV,)),
        pltpu.SemaphoreType.DMA((6,)),
    ]
    in_vmem = pl.BlockSpec(memory_space=pltpu.VMEM)
    anywhere = pl.BlockSpec(memory_space=pl.ANY)
    in_hbm = pl.BlockSpec(memory_space=pltpu.HBM)
    shapes = (
        jax.ShapeDtypeStruct((4, 64, 512), BF),
        jax.ShapeDtypeStruct((4, 64, 512), BF),
        jax.ShapeDtypeStruct((64, 512), F32),
        jax.ShapeDtypeStruct((256, 4096), BF),
        jax.ShapeDtypeStruct((256, 4096), BF),
    )
    results = pl.pallas_call(
        kernel,
        out_shape=shapes,
        in_specs=[in_hbm] * 6,
        out_specs=[in_vmem] * 5,
        scratch_shapes=scratch,
        compiler_params=pltpu.CompilerParams(
            collective_id=0, has_side_effects=True, vmem_limit_bytes=44 * 1024 * 1024),
        cost_estimate=pl.CostEstimate(flops=4 * 10**9, bytes_accessed=10**7, transcendentals=10**5),
    )(*[pltpu.with_memory_space_constraint(a, pltpu.HBM)
        for a in (tokens, cotangent, groups, router.T, w_in, w_out)])
    mixed_out, tokens_grad, router_t, g_in, g_out = pl.pallas_call(
        copy_out,
        out_shape=shapes,
        in_specs=[anywhere] * 5,
        out_specs=[anywhere] * 5,
        scratch_shapes=[pltpu.SemaphoreType.DMA((5,))],
        compiler_params=pltpu.CompilerParams(vmem_limit_bytes=2 * 1024 * 1024),
    )(*results)
    return mixed_out, tokens_grad, router_t.T, g_in, g_out


def solution(mesh):
    return jax.shard_map(
        per_device,
        mesh=mesh,
        in_specs=(
            P("dp", None, "mp"),
            P("dp", None),
            P("mp", None),
            P(("mp", "dp"), None),
            P(("mp", "dp"), None),
            P("dp", None, "mp"),
        ),
        out_specs=(
            P("dp", None, "mp"),
            P("dp", None, "mp"),
            P("mp", None),
            P(("mp", "dp"), None),
            P(("mp", "dp"), None),
        ),
        check_vma=False,
    )
```
